256 devices in a mesh: gz: 64 (over y, z, core), xy: 4 (over x).
Axes of the slice: x: 4, y: 4, z: 8, core: 2. Of those that a mesh axis runs over, the one named last changes fastest.
Arguments:
- sections: bfloat16 [256, 512, 2048], P('gz', 'xy'), may hold values from -16 to 16
- skips: int32 [256, 2], P('gz'), may hold values from 0 to 3, as said below
- patch_valid: int32 [256, 8, 32], P('gz', 'xy'), may hold values 0 or 1
- velocity_start: float32 [256, 2, 8, 32], P('gz', None, 'xy'), may hold values from -8 to 8
- step_size: float32 [3], replicated, may hold values from 0.15 to 0.45
- mixing: float32 [3], replicated, may hold values from 0.1 to 0.6
Outputs:
- flow_field: float32 [256, 2, 2, 8, 32], P('gz', None, None, 'xy')
- displace: float32 [256, 2, 8, 32], P('gz', None, 'xy')
The draws below stay inside these ranges and needn't reach their ends.
Inputs may be any that keep to these rules, and one draw needn't show every extreme that they name: `skips`: entry 0 of a row is the first partner's distance, 1 to 3; entry 1 is 0 where there is no second partner, else a distance of 1 to 3 other than entry 0. Some row has distance 3.
All inputs are finite; a program needn't handle non-finite values. No bound on the sum of `patch_valid` on one device may be relied on, other than what follows from the above.
Results may differ from the reference program's by a relative error of at most 0.0014.
Values may be sent and summed in bfloat16 or wider, within the bound.
A program may use at most 128 MiB of HBM per device.

```python
import math
import jax
import jax.numpy as jnp
from jax import lax

PATCH = 64
REACH = 3
ITERS = 3
W = 2048
NS = 256
H = 512
PH = 8
PW = 32


def draw_sections(key, part):
    key = jax.random.fold_in(key, 5)
    base_key, offset_key, noise_key, level_key = jax.random.split(key, 4)
    margin = 8
    patch_rows = H // PATCH
    patch_cols = W // PATCH
    field = jax.random.normal(base_key, (H + margin, W + margin), jnp.float32)
    field = (field + 0.7 * jnp.roll(field, 1, 0) + 0.7 * jnp.roll(field, 1, 1)) * 0.7
    offsets = jax.random.randint(offset_key, (2, NS, patch_rows, patch_cols), 0, margin)
    levels = jnp.exp(jax.random.uniform(level_key, (NS, patch_rows, patch_cols), jnp.float32, jnp.log(0.3), jnp.log(3.0)))
    row_ids = jnp.arange(H, dtype=jnp.int32)
    col_ids = jnp.arange(W, dtype=jnp.int32)
    noise_keys = jax.random.split(noise_key, NS)

    def one_section(section_args):
        off_rows, off_cols, level_grid, section_key = section_args
        row_index = row_ids[:, None] + jnp.repeat(jnp.repeat(off_rows, PATCH, 0), PATCH, 1)
        col_index = col_ids[None, :] + jnp.repeat(jnp.repeat(off_cols, PATCH, 0), PATCH, 1)
        picture = field[row_index, col_index]
        level_full = jnp.repeat(jnp.repeat(level_grid, PATCH, 0), PATCH, 1)
        noise_field = jax.random.normal(section_key, (H, W), jnp.float32)
        return jnp.clip(picture + level_full * noise_field, -16.0, 16.0)
    pictures = lax.map(one_section, (offsets[0], offsets[1], levels, noise_keys))
    return pictures.astype(jnp.bfloat16)


def draw_skips(key, part):
    key = jax.random.fold_in(key, 9)
    first_key, extra_key, second_key = jax.random.split(key, 3)
    leading = jax.random.randint(first_key, (NS,), 1, REACH + 1)
    leading = leading.at[0].set(REACH)
    other = (leading - 1 + jax.random.randint(extra_key, (NS,), 1, REACH)) % REACH + 1
    has_second = jax.random.randint(second_key, (NS,), 0, 2)
    return jnp.stack([leading, other * has_second], axis=1).astype(jnp.int32)


def draw_velocity_start(key, part):
    key = jax.random.fold_in(key, 13)
    scale_key, noise_key = jax.random.split(key, 2)
    patch_rows = H // PATCH
    patch_cols = W // PATCH
    scales = jnp.exp(jax.random.uniform(scale_key, (NS, 1, 1, 1), jnp.float32, jnp.log(0.3), jnp.log(3.0)))
    values = scales * jax.random.normal(noise_key, (NS, 2, patch_rows, patch_cols), jnp.float32)
    return jnp.clip(values, -8.0, 8.0)


def touch_ends(entries, own_key, low, high):
    longest = entries.shape.index(max(entries.shape))
    spots = []
    for shift in (0, 1):
        where = [jax.random.randint(jax.random.fold_in(own_key, axis), (), 0, length) for axis, length in enumerate(entries.shape)]
        where[longest] = (where[longest] + shift) % entries.shape[longest]
        spots.append(tuple(where))
    return entries.at[spots[0]].set(low).at[spots[1]].set(high)


def setup_inputs(seed: int = 0) -> dict:
    key_of = jax.random.split(jax.random.key(seed), 7)
    sections = draw_sections(jax.random.fold_in(key_of[6], 71), 0)
    skips = draw_skips(jax.random.fold_in(key_of[6], 71), 0)
    patch_valid = touch_ends((jax.random.randint(key_of[2], (NS, PH, PW), 0, 8) < 7).astype(jnp.int32), jax.random.fold_in(key_of[2], 1), 0, 1)
    velocity_start = draw_velocity_start(jax.random.fold_in(key_of[6], 71), 0)
    step_size = jnp.clip(jnp.exp(jax.random.uniform(key_of[4], (ITERS,), jnp.float32, math.log(0.15), math.log(0.45))), 0.15, 0.45)
    mixing = jnp.clip(jax.random.uniform(key_of[5], (ITERS,), jnp.float32, 0.1, 0.6), 0.1, 0.6)
    return {"sections": sections, "skips": skips, "patch_valid": patch_valid, "velocity_start": velocity_start, "step_size": step_size, "mixing": mixing}


SHARP = 400.0
STIFF = 0.25
TINY = 1e-06

def tables():
    indices = jnp.arange(PATCH, dtype=jnp.int32)
    phases = indices[:, None] * indices[None, :] % PATCH
    angles = phases.astype(jnp.float32) * (2.0 * jnp.pi / PATCH)
    cosine = jnp.cos(angles)
    sines = jnp.sin(angles)
    forward_cols = jnp.concatenate([cosine, sines], axis=1).astype(jnp.bfloat16)
    forward_rows = jnp.concatenate([cosine, sines], axis=0).astype(jnp.bfloat16)
    inverse_cols = jnp.concatenate([jnp.concatenate([cosine, sines], axis=1), jnp.concatenate([-sines, cosine], axis=1)], axis=0).astype(jnp.bfloat16)
    inverse_rows = jnp.stack([cosine, -sines], axis=1).astype(jnp.bfloat16)
    shifts = jnp.where(indices < PATCH // 2, indices, indices - PATCH).astype(jnp.float32)
    return (forward_cols, forward_rows, inverse_cols, inverse_rows, shifts)

def spectra(image_tile, forward_cols, forward_rows):
    patch_rows = image_tile.shape[0] // PATCH
    patch_cols = image_tile.shape[1] // PATCH
    blocks = image_tile.astype(jnp.float32).reshape(patch_rows, PATCH, patch_cols, PATCH)
    centred = blocks - lax.optimization_barrier(jnp.mean(blocks, axis=(1, 3), keepdims=True))
    spread = lax.optimization_barrier(jnp.mean(centred * centred, axis=(1, 3), keepdims=True))
    normed = (centred * lax.rsqrt(spread + 1e-05)).astype(jnp.bfloat16)
    halfway = jnp.einsum('anbm,mc->anbc', normed.astype(jnp.float32), forward_cols.astype(jnp.float32)).astype(jnp.bfloat16)
    combined = jnp.einsum('kn,anbc->abkc', forward_rows.astype(jnp.float32), halfway.astype(jnp.float32))
    cos_part = combined[:, :, :PATCH, :]
    sin_part = combined[:, :, PATCH:, :]
    real_part = cos_part[..., :PATCH] - sin_part[..., PATCH:]
    imag_part = -(sin_part[..., :PATCH] + cos_part[..., PATCH:])
    return jnp.concatenate([real_part, imag_part], axis=-1).astype(jnp.bfloat16)

def soft_flow(spec_self, partners, inverse_cols, inverse_rows, shifts):
    spec_mine = spec_self.astype(jnp.float32)[:, :, :, None, :]
    spec_other = partners.astype(jnp.float32)
    real_self = spec_mine[..., :PATCH]
    imag_self = spec_mine[..., PATCH:]
    real_other = spec_other[..., :PATCH]
    imag_other = spec_other[..., PATCH:]
    cross_spec = jnp.concatenate([real_self * real_other + imag_self * imag_other, real_self * imag_other - imag_self * real_other], axis=-1).astype(jnp.bfloat16)
    inverse_half = jnp.einsum('abkjc,cd->abkjd', cross_spec.astype(jnp.float32), inverse_cols.astype(jnp.float32)).astype(jnp.bfloat16)
    shape_now = inverse_half.shape
    inverse_half = inverse_half.reshape(shape_now[0], shape_now[1], PATCH, shape_now[3], 2, PATCH)
    correlation = jnp.einsum('trk,abkjrc->abtjc', inverse_rows.astype(jnp.float32), inverse_half.astype(jnp.float32))
    scores = correlation * (SHARP / float(PATCH ** 4))
    peak_score = lax.optimization_barrier(jnp.max(scores, axis=(2, 4), keepdims=True))
    soft_weights = jnp.exp(scores - peak_score)
    total_sum = lax.optimization_barrier(jnp.sum(soft_weights, axis=(2, 4)))
    along_rows = lax.optimization_barrier(jnp.sum(soft_weights * shifts[None, None, :, None, None], axis=(2, 4))) / total_sum
    along_cols = lax.optimization_barrier(jnp.sum(soft_weights * shifts[None, None, None, None, :], axis=(2, 4))) / total_sum
    return jnp.transpose(jnp.stack([along_rows, along_cols], axis=0), (3, 0, 1, 2))

def inplane(displace):
    padded = jnp.pad(displace, ((0, 0), (0, 0), (1, 1), (1, 1)))
    return STIFF * (padded[:, :, 2:, 1:-1] + padded[:, :, :-2, 1:-1] + padded[:, :, 1:-1, 2:] + padded[:, :, 1:-1, :-2] - 4.0 * displace)

def reference(sections, skips, patch_valid, velocity_start, step_size, mixing):
    forward_cols, forward_rows, inverse_cols, inverse_rows, shifts = tables()
    sections_all = sections.shape[0]
    patch_rows = sections.shape[1] // PATCH
    patch_cols = sections.shape[2] // PATCH
    section_ids = jnp.arange(sections_all, dtype=jnp.int32)
    zero_window = jnp.zeros((REACH, patch_rows, patch_cols, PATCH, 2 * PATCH), jnp.bfloat16)

    def visit_section(window, section_item):
        image_tile, skip_row, position = section_item
        own_spec = spectra(image_tile, forward_cols, forward_rows)
        ahead_specs = jnp.concatenate([own_spec[None], window], axis=0)
        partners = jnp.stack([ahead_specs[skip_row[0]], ahead_specs[skip_row[1]]], axis=3)
        pair_flow = soft_flow(own_spec, partners, inverse_cols, inverse_rows, shifts)
        paired = (skip_row > 0) & (position + skip_row < sections_all)
        pair_flow = jnp.where(paired[:, None, None, None], pair_flow, 0.0)
        return (ahead_specs[:REACH], pair_flow)
    unused_window, flow_field = lax.scan(visit_section, zero_window, (sections, skips, section_ids), reverse=True)
    valid_mask = patch_valid.astype(jnp.float32)
    target = jnp.clip(section_ids[:, None] + skips, 0, sections_all - 1).astype(jnp.int32)
    paired = ((skips > 0) & (section_ids[:, None] + skips < sections_all)).astype(jnp.float32)
    weight = paired[:, :, None, None] * valid_mask[:, None] * valid_mask[target]
    displace = jnp.zeros((sections_all, 2, patch_rows, patch_cols), jnp.float32)
    velocity = velocity_start.astype(jnp.float32)
    for iteration in range(ITERS):
        partner = displace[target]
        tension = weight[:, :, None] * (partner - displace[:, None] - flow_field)
        pushed = jax.ops.segment_sum(tension.reshape(sections_all * 2, 2, patch_rows, patch_cols), target.reshape(-1), sections_all)
        forces = inplane(displace) + lax.optimization_barrier(jnp.sum(tension, axis=1)) - pushed
        power_sum = jnp.sum(forces * velocity)
        speed_sum = jnp.sum(velocity * velocity)
        strength = jnp.sum(forces * forces)
        gating = 0.5 + 0.5 * power_sum / jnp.sqrt((speed_sum + TINY) * (strength + TINY))
        scale_ratio = jnp.sqrt((speed_sum + TINY) / (strength + TINY))
        velocity = gating * ((1.0 - mixing[iteration]) * velocity + mixing[iteration] * scale_ratio * forces)
        velocity = velocity + step_size[iteration] * forces
        displace = displace + step_size[iteration] * velocity
    return (flow_field, displace)
```

```python
import functools
import jax
import jax.numpy as jnp
import numpy as np
import ml_dtypes
from jax import lax
from jax.experimental import pallas as pl
from jax.experimental.pallas import tpu as pltpu
from jax.sharding import PartitionSpec as P

PATCH = 64
HALF = 32
REACH = 3
SHARP = 400.0
SCORE_SCALE = SHARP / float(PATCH**4)
LOG2E = 1.4426950408889634
VM = pl.BlockSpec(memory_space=pltpu.VMEM)
SM = pl.BlockSpec(memory_space=pltpu.SMEM)


def host_tables():
    n = np.arange(PATCH)
    angle = ((n[:, None] * n[None, :]) % PATCH) * (2.0 * np.pi / PATCH)
    rounded = lambda a: np.where(np.abs(a) < 1e-9, 0.0, a).astype(ml_dtypes.bfloat16).astype(np.float64)
    cos, sin = rounded(np.cos(angle)), rounded(np.sin(angle))
    z = np.zeros((PATCH, PATCH))
    forward_cols = np.block([[cos, z, sin, z], [z, cos, z, sin]])
    forward_rows = np.concatenate([cos[:32], cos[32:33], sin[1:32]], axis=0)

    def couple(rr, ri, ir, ii):
        return np.block([[rr, z, ri, z], [z, rr, z, ri], [ir, z, ii, z], [z, ir, z, ii]])

    icols = couple(cos, sin, -sin, cos)
    rr, ri, ir, ii = (np.zeros((PATCH, PATCH)) for _ in range(4))
    rr[0] = cos[0]
    rr[1:32] = 2.0 * cos[1:32]
    ir[1:32] = -2.0 * sin[1:32]
    ir[0] = cos[32]
    ri[32] = cos[32]
    ri[33:] = 2.0 * cos[33:]
    ii[33:] = -2.0 * sin[33:]
    ii[32] = cos[0]
    ipack = couple(rr, ri, ir, ii)
    rows = np.zeros((64, 64))
    rows[:, 0] = 1.0
    rows[:, 1:32] = 2.0 * cos[:, 1:32]
    rows[:, 32] = cos[:, 32]
    rows[:, 33:] = -2.0 * sin[:, 1:32]
    spread = np.zeros((2, 64, 128))
    for half in range(2):
        for a in range(2):
            for j in range(2):
                for c in range(16):
                    spread[half, a * 32 + j * 16 + c, j * 64 + a * 32 + 2 * c + half] = 1.0
    bf = lambda a: a.astype(ml_dtypes.bfloat16)
    return dict(fcols=bf(forward_cols), frows=bf(forward_rows), icols=bf(icols), ipack=bf(ipack), irows=bf(rows),
                spread=spread.reshape(128, 128).astype(np.float32))


def half_sums(v, left):
    a = jnp.sum(jnp.where(left, v, 0.0), axis=1, keepdims=True)
    b = jnp.sum(jnp.where(left, 0.0, v), axis=1, keepdims=True)
    return jnp.where(left, a, b)


def tile_stats(x_ref, s, a, mean_ref, rs_ref, width, chunk=512):
    rows = pl.ds(pl.multiple_of(a * PATCH, PATCH), PATCH)
    left = lax.broadcasted_iota(jnp.int32, (1, 128), 1) < 64
    t = s * 2 + a
    scale = 1.0 / PATCH**2
    for c in range(0, width, chunk):
        x = x_ref[s, rows, c:c + chunk].astype(jnp.float32)
        total = jnp.sum(x, axis=0, keepdims=True)
        mean = jnp.concatenate([half_sums(total[:, k:k + 128], left) for k in range(0, chunk, 128)], axis=1) * scale
        mean_ref[t, :, c:c + chunk] = mean
        d = x - mean
        total = jnp.sum(d * d, axis=0, keepdims=True)
        spread = jnp.concatenate([half_sums(total[:, k:k + 128], left) for k in range(0, chunk, 128)], axis=1) * scale
        rs_ref[t, :, c:c + chunk] = lax.rsqrt(spread + 1e-5)


def forward_cols_step(x_ref, s, a, g, groups, mean_ref, rs_ref, fcols, half_ref):
    rows = pl.ds(pl.multiple_of(a * PATCH, PATCH), PATCH)
    t = s * 2 + a
    for i in range(groups):
        cols = pl.ds(pl.multiple_of((g + i) * 128, 128), 128)
        x = x_ref[s, rows, cols].astype(jnp.float32)
        normed = ((x - mean_ref[t, :, cols]) * rs_ref[t, :, cols]).astype(jnp.bfloat16)
        half_ref[:, i * 256:(i + 1) * 256] = jnp.dot(normed, fcols, preferred_element_type=jnp.float32).astype(jnp.bfloat16)


def forward_rows_step(s, a, g, groups, frows, half_ref, spec_ref):
    lane = lax.broadcasted_iota(jnp.int32, (8, 128), 1) % 64
    row0 = lax.broadcasted_iota(jnp.int32, (8, 128), 0) == 0
    upper = lane >= 32
    for i in range(groups):
        both = jnp.dot(frows, half_ref[:, i * 256:(i + 1) * 256], preferred_element_type=jnp.float32)
        ca, cb = both[:HALF, :128], both[:HALF, 128:]
        sa, sb = both[HALF:, :128], both[HALF:, 128:]
        real, imag = ca - sb, sa + cb
        ca, cb, sa, sb = ca[:8], cb[:8], sa[:8], sb[:8]
        real0 = jnp.where(upper, sa, ca)
        imag0 = jnp.where(upper, sb, cb)
        imag0 = jnp.where(lane == 0, pltpu.roll(ca, 96, axis=1), jnp.where(lane == 32, pltpu.roll(sa, 32, axis=1), imag0))
        real = jnp.concatenate([jnp.where(row0, real0, real[:8]), real[8:]], axis=0)
        imag = jnp.concatenate([jnp.where(row0, imag0, imag[:8]), imag[8:]], axis=0)
        spec_ref[s, a, g + i] = jnp.concatenate([real, imag], axis=1).astype(jnp.bfloat16)


def forward_all(x_ref, tiles, mean_ref, rs_ref, fcols_ref, frows_ref, half_ref, spec_ref, width):
    groups = width // 128
    count = x_ref.shape[0] * 2

    def stats(i):
        s, a = tiles(i)
        tile_stats(x_ref, s, a, mean_ref, rs_ref, width)

    def columns(i):
        s, a = tiles(i)
        forward_cols_step(x_ref, s, a, 0, groups, mean_ref, rs_ref, fcols_ref[...], half_ref)

    def rows(i):
        s, a = tiles(i)
        forward_rows_step(s, a, 0, groups, frows_ref[...], half_ref, spec_ref)

    stats(0)
    stats(1)
    columns(0)

    def step(i, _):
        rows(i - 2)
        columns(i - 1)
        stats(i)
        return 0

    lax.fori_loop(2, count, step, 0)
    rows(count - 2)
    columns(count - 1)
    rows(count - 1)


def pair_cross(spec_ref, s, a, c, count, partner, icols, ipack, u_ref):
    lane = lax.broadcasted_iota(jnp.int32, (8, 128), 1) % 32
    row = lax.broadcasted_iota(jnp.int32, (8, 128), 0)
    special = (row == 0) & (lane == 0)
    blocks = []
    for i in range(count):
        mine = spec_ref[s, a, c + i].astype(jnp.float32)
        r, m = mine[:, :128], mine[:, 128:]
        for j in range(2):
            other = spec_ref[partner[j], a, c + i].astype(jnp.float32)
            p, q = other[:, :128], other[:, 128:]
            rp, mq = r * p, m * q
            real, imag = rp + mq, m * p - r * q
            real = jnp.concatenate([jnp.where(special, rp[:8], real[:8]), real[8:]], axis=0)
            imag = jnp.concatenate([jnp.where(special, mq[:8], imag[:8]), imag[8:]], axis=0)
            blocks.append(jnp.concatenate([real, imag], axis=1).astype(jnp.bfloat16))
    n = len(blocks)
    inner = jnp.dot(jnp.concatenate(blocks, axis=0), icols, preferred_element_type=jnp.float32)
    first = jnp.dot(jnp.concatenate([b[:16] for b in blocks], axis=0), ipack, preferred_element_type=jnp.float32)
    row0 = lax.broadcasted_iota(jnp.int32, (8, 256), 0) == 0
    for i in range(n):
        head = jnp.where(row0, first[i * 16:i * 16 + 8], inner[i * 32:i * 32 + 8])
        u = jnp.concatenate([head, inner[i * 32 + 8:i * 32 + 32]], axis=0).astype(jnp.bfloat16)
        u_ref[:32, i * 128:(i + 1) * 128] = u[:, :128]
        u_ref[32:, i * 128:(i + 1) * 128] = u[:, 128:]


def pair_soft(u_ref, n, irows, m_ref, z_ref, r_ref, base):
    for h in range(0, n, 2):
        corr = jnp.dot(irows, u_ref[:, h * 128:(h + 2) * 128], preferred_element_type=jnp.float32)
        for i in (h, h + 1):
            e = [corr[8 * r:8 * r + 8, (i - h) * 128:(i - h + 1) * 128] for r in range(8)]
            m = functools.reduce(jnp.maximum, e)
            e = [jnp.exp2((v - m) * (SCORE_SCALE * LOG2E)) for v in e]
            s3 = e[3]
            s2 = e[2] + s3
            s1 = e[1] + s2
            t4 = e[4]
            t5 = t4 + e[5]
            t6 = t5 + e[6]
            t7 = t6 + e[7]
            spot = pl.ds(pl.multiple_of((base + (i % 2) * 16 + i // 2) * 8, 8), 8)
            m_ref[spot] = m
            z_ref[spot] = (s1 + e[0]) + t7
            r_ref[spot] = ((s1 + s2) + s3) - ((t4 + t5) + (t6 + t7))


def pair_finish(m_ref, z_ref, r_ref, spread_ref):
    rows = m_ref.shape[0] // 8
    lane = lax.broadcasted_iota(jnp.int32, (rows, 128), 1)
    left = lane < 64
    t2 = lane % 64
    shift = jnp.where(t2 < 32, t2, t2 - 64).astype(jnp.float32)
    pick = lambda ref, r: ref[pl.ds(r, rows, stride=8), :]
    top = functools.reduce(jnp.maximum, [pick(m_ref, r) for r in range(8)])
    a = jnp.max(jnp.where(left, top, -jnp.inf), axis=1, keepdims=True)
    b = jnp.max(jnp.where(left, -jnp.inf, top), axis=1, keepdims=True)
    peak = jnp.where(left, a, b)
    total = jnp.zeros((rows, 128), jnp.float32)
    along = jnp.zeros((rows, 128), jnp.float32)
    for r in range(8):
        w = jnp.exp2((pick(m_ref, r) - peak) * (SCORE_SCALE * LOG2E))
        z = pick(z_ref, r)
        total += w * z
        along += w * (8.0 * pick(r_ref, r) + float(r) * z)
    sel = (lax.broadcasted_iota(jnp.int32, (8, 128), 1) // 64 == lax.broadcasted_iota(jnp.int32, (8, 128), 0)).astype(jnp.float32)
    exact = dict(precision=lax.Precision.HIGHEST, preferred_element_type=jnp.float32)
    nt = lambda v: lax.dot_general(sel, v, (((1,), (1,)), ((), ())), **exact)
    tot = nt(total)
    f = [nt(along) / tot, nt(total * shift) / tot]
    both = jnp.concatenate([jnp.concatenate([v[0:1], v[1:2]], axis=1) for v in f] + [jnp.zeros((6, 128), jnp.float32)], axis=0)
    return jnp.dot(both, spread_ref[...], **exact)


def pair_section(spec_ref, s, partner, icols_ref, ipack_ref, irows_ref, spread_ref, u_ref, m_ref, z_ref, r_ref, count=16):
    per = 16 // count
    n = 2 * count

    def cross(i):
        pair_cross(spec_ref, s, i // per, (i % per) * count, count, partner, icols_ref[...], ipack_ref[...], u_ref)

    def soft(i):
        pair_soft(u_ref, n, irows_ref[...], m_ref, z_ref, r_ref, (i // per) * 32 + (i % per) * count)

    cross(0)

    def step(i, _):
        soft(i - 1)
        cross(i)
        return 0

    lax.fori_loop(1, 2 * per, step, 0)
    soft(2 * per - 1)
    return pair_finish(m_ref, z_ref, r_ref, spread_ref)


def emit_flow(s, flow, skip_ref, live_ref, valid_ref, start_ref, flow_ref, pay_ref):
    skip = [skip_ref[s, 0], skip_ref[s, 1]]
    live = [live_ref[s, 0] > 0, live_ref[s, 1] > 0]
    here = [jnp.where(live[j], jnp.concatenate([flow[c:c + 1, j * 64:(j + 1) * 64] for c in range(2)], axis=1), 0.0) for j in range(2)]
    for c in range(2):
        for a in range(2):
            spot = c * 64 + a * 32
            for j in range(2):
                flow_ref[s, j, c, a:a + 1, :] = here[j][:, spot:spot + 32]
    good = jnp.concatenate([valid_ref[s, a:a + 1, :] for _ in range(2) for a in range(2)], axis=1).astype(jnp.float32)
    start = jnp.concatenate([start_ref[s, c, a:a + 1, :] for c in range(2) for a in range(2)], axis=1)
    pay_ref[0, s:s + 1, :] = start
    pay_ref[1, s:s + 1, :] = good
    for d in (1, 2, 3):
        hit = [(skip[j] == d) & live[j] for j in range(2)]
        pay_ref[1 + d, s:s + 1, :] = jnp.where(hit[0] | hit[1], good, 0.0)
        pay_ref[4 + d, s:s + 1, :] = jnp.where(hit[0], here[0], jnp.where(hit[1], here[1], 0.0))


def forward_kernel(x_ref, fcols_ref, frows_ref, spec_ref, mean_ref, rs_ref, half_ref):
    forward_all(x_ref, lambda i: (i // 2, i % 2), mean_ref, rs_ref, fcols_ref, frows_ref, half_ref, spec_ref, x_ref.shape[2])


def forward_call(x, tb):
    s, _, width = x.shape
    return pl.pallas_call(
        forward_kernel,
        out_shape=jax.ShapeDtypeStruct((s, 2, width // 128, HALF, 256), jnp.bfloat16),
        in_specs=[VM] * 3, out_specs=VM,
        scratch_shapes=[pltpu.VMEM((2 * s, 1, width), jnp.float32)] * 2 + [pltpu.VMEM((64, 4096), jnp.bfloat16)],
        compiler_params=pltpu.CompilerParams(vmem_limit_bytes=48 * 2**20),
        name="forward",
    )(x, tb["fcols"], tb["frows"])


def pair_kernel(target_ref, skip_ref, live_ref, valid_ref, start_ref, spec_ref, icols_ref, ipack_ref, irows_ref, spread_ref,
                flow_ref, pay_ref, u_ref, m_ref, z_ref, r_ref):
    for s in range(flow_ref.shape[0]):
        flow = pair_section(spec_ref, s, (target_ref[s, 0], target_ref[s, 1]), icols_ref, ipack_ref, irows_ref, spread_ref,
                            u_ref, m_ref, z_ref, r_ref)
        emit_flow(s, flow, skip_ref, live_ref, valid_ref, start_ref, flow_ref, pay_ref)


def pair_call(target, skips, live, valid, start, spec, tb):
    sections = target.shape[0]
    return pl.pallas_call(
        pair_kernel,
        out_shape=(jax.ShapeDtypeStruct((sections, 2, 2, 2, 32), jnp.float32),
                   jax.ShapeDtypeStruct((8, sections, 128), jnp.float32)),
        in_specs=[SM] * 3 + [VM] * 7, out_specs=(VM, VM),
        scratch_shapes=[pltpu.VMEM((64, 4096), jnp.bfloat16)] + [pltpu.VMEM((512, 128), jnp.float32)] * 3,
        compiler_params=pltpu.CompilerParams(vmem_limit_bytes=48 * 2**20),
        name="pairs",
    )(target, skips, live, valid, start, spec, tb["icols"], tb["ipack"], tb["irows"], tb["spread"])


TINY = 1e-06
STIFF = 0.25
ITERS = 3
FIELDS = 8
BEFORE, AFTER = 3, 3
MESH = pl.DeviceIdType.MESH


def shifted(x, by):
    n = x.shape[0]
    return pltpu.roll(x, (-by) % n, axis=0)


def relax_kernel(nz, nx, step_ref, mix_ref, pay_ref, out_ref, ext, part1, part2, sem_a, got_a, sem_1, got_1, sem_2, got_2):
    gz = lax.axis_index("gz")
    xy = lax.axis_index("xy")
    groups = nz // 4
    yy, zc = gz // groups, gz % groups
    halo = [(db, dx) for db in range(-BEFORE, AFTER + 1) for dx in (-1, 0, 1) if (db, dx) != (0, 0)]

    def at(db, dx):
        return (lax.rem(gz + db + nz, nz), lax.rem(xy + dx + nx, nx))

    def near(r):
        k = lax.rem(yy * nx + xy + r, 4 * nx)
        return (k // nx * groups + zc, lax.rem(k, nx))

    def along(r):
        return (yy * groups + lax.rem(zc + r, groups), xy)

    barrier = pltpu.get_barrier_semaphore()
    for db, dx in halo:
        pl.semaphore_signal(barrier, inc=1, device_id=at(db, dx), device_id_type=MESH)
    for r in range(1, 4 * nx):
        pl.semaphore_signal(barrier, inc=1, device_id=near(r), device_id_type=MESH)
    for r in range(1, groups):
        pl.semaphore_signal(barrier, inc=1, device_id=along(r), device_id_type=MESH)
    pl.semaphore_wait(barrier, len(halo) + 4 * nx - 1 + groups - 1)

    copies = []
    for n, (db, dx) in enumerate(halo):
        copies.append(pltpu.make_async_remote_copy(
            src_ref=pay_ref, dst_ref=ext.at[dx + 1, db + BEFORE], send_sem=sem_a.at[n], recv_sem=got_a.at[n],
            device_id=at(-db, -dx), device_id_type=MESH))
        copies[-1].start()
    ext[1, BEFORE] = pay_ref[...]
    for c in copies:
        c.wait()

    blocks = BEFORE + AFTER + 1
    own = slice(4 * BEFORE, 4 * BEFORE + 4)
    lane = lax.broadcasted_iota(jnp.int32, (4 * blocks + 4, 128), 1)
    col = lane % 32
    upper = (lane // 32) % 2 == 0
    inside = [jnp.where(xy > 0, 1.0, 0.0), 1.0, jnp.where(xy < nx - 1, 1.0, 0.0)]

    def field(dx, f):
        return jnp.concatenate([ext[dx, k, f] for k in range(blocks)] + [jnp.zeros((4, 128), jnp.float32)], axis=0)

    vel, bias, weights = [], [], []
    for dx in range(3):
        valid = field(dx, 1)
        total = jnp.zeros_like(valid)
        ws = []
        for d in (1, 2, 3):
            w = field(dx, 1 + d) * shifted(valid, d)
            wf = w * field(dx, 4 + d)
            total += shifted(wf, -d) - wf
            ws.append(w)
        weights.append(ws)
        bias.append(total * inside[dx])
        vel.append(field(dx, 0) * inside[dx])

    def force(fields, dx):
        v = fields[dx]
        above = fields[dx - 1] if dx > 0 else jnp.zeros_like(v)
        below = fields[dx + 1] if dx < 2 else jnp.zeros_like(v)
        lateral = jnp.where(col == 0, 0.0, pltpu.roll(v, 1, axis=1)) + jnp.where(col == 31, 0.0, pltpu.roll(v, 127, axis=1))
        down, up = pltpu.roll(v, 32, axis=1), pltpu.roll(v, 96, axis=1)
        vertical = jnp.where(upper, pltpu.roll(above, 96, axis=1) + up, down + pltpu.roll(below, 32, axis=1))
        out = STIFF * (lateral + vertical - 4.0 * v)
        for d in (1, 2, 3):
            pull = weights[dx][d - 1] * (shifted(v, d) - v)
            out += pull - shifted(pull, -d)
        return out * inside[dx]

    av = [force(vel, dx) for dx in range(3)]
    ab = [force(bias, dx) for dx in range(3)]
    aav, aab = force(av, 1), force(ab, 1)
    basis = [x[own] for x in (vel[1], bias[1], av[1], ab[1], aav, aab)]

    index = {}
    rows = []
    for i in range(6):
        for j in range(i, 6):
            index[i, j] = index[j, i] = len(rows)
            rows.append(jnp.sum(basis[i] * basis[j], axis=0, keepdims=True))
    rows += [jnp.zeros_like(rows[0])] * 3
    part1[0] = jnp.concatenate(rows, axis=0)

    def reduce(part, count, peer, sem, got):
        sends = []
        for r in range(1, count):
            sends.append(pltpu.make_async_remote_copy(
                src_ref=part.at[0], dst_ref=part.at[r], send_sem=sem.at[r], recv_sem=got.at[r],
                device_id=peer(r), device_id_type=MESH))
            sends[-1].start()
        for c in sends:
            c.wait()
        return functools.reduce(jnp.add, [part[r] for r in range(count)])

    part2[0] = reduce(part1, 4 * nx, near, sem_1, got_1)
    gram = jnp.sum(reduce(part2, groups, along, sem_2, got_2), axis=1, keepdims=True)
    gram = jnp.broadcast_to(gram, (24, 128))
    g = {k: gram[n:n + 1] for k, n in index.items()}

    def dot(p, q):
        terms = [p[i] * q[j] * g[i, j] for i in range(6) for j in range(6) if p[i] is not None and q[j] is not None]
        return functools.reduce(jnp.add, terms)

    def plus(*xs):
        xs = [x for x in xs if x is not None]
        return functools.reduce(jnp.add, xs) if xs else None

    def times(k, x):
        return None if x is None else k * x

    one = jnp.ones((1, 128), jnp.float32)
    v = [one] + [None] * 5
    d = [None] * 6
    for it in range(ITERS):
        f = [None, one] + d[:4]
        power, speed, strength = dot(f, v), dot(v, v), dot(f, f)
        speed, strength = jnp.maximum(speed, 0.0), jnp.maximum(strength, 0.0)
        gating = 0.5 + 0.5 * power / jnp.sqrt((speed + TINY) * (strength + TINY))
        ratio = jnp.sqrt((speed + TINY) / (strength + TINY))
        mix, step = mix_ref[it], step_ref[it]
        kv, kf = gating * (1.0 - mix), gating * (mix * ratio) + step
        v = [plus(times(kv, v[i]), times(kf, f[i])) for i in range(6)]
        d = [plus(d[i], times(step, v[i])) for i in range(6)]
    result = functools.reduce(jnp.add, [d[i] * basis[i] for i in range(6)])
    for c in range(2):
        for a in range(2):
            at0 = c * 64 + a * 32
            for s in range(4):
                out_ref[s, c, a:a + 1, :] = result[s:s + 1, at0:at0 + 32]


def relax_call(step, mix, payload, nz, nx):
    vm = pl.BlockSpec(memory_space=pltpu.VMEM)
    sm = pl.BlockSpec(memory_space=pltpu.SMEM)
    dma = pltpu.SemaphoreType.DMA
    blocks = BEFORE + AFTER + 1
    return pl.pallas_call(
        functools.partial(relax_kernel, nz, nx),
        out_shape=jax.ShapeDtypeStruct((4, 2, 2, 32), jnp.float32),
        in_specs=[sm, sm, vm], out_specs=vm,
        scratch_shapes=[
            pltpu.VMEM((3, blocks, FIELDS, 4, 128), jnp.float32),
            pltpu.VMEM((4 * nx, 24, 128), jnp.float32),
            pltpu.VMEM((nz // 4, 24, 128), jnp.float32),
            dma((3 * blocks,)), dma((3 * blocks,)), dma((4 * nx,)), dma((4 * nx,)), dma((nz // 4,)), dma((nz // 4,)),
        ],
        compiler_params=pltpu.CompilerParams(collective_id=0, has_side_effects=True, vmem_limit_bytes=32 * 2**20),
        name="relax",
    )(step, mix, payload)


def body(sections, skips, patch_valid, velocity_start, step_size, mixing):
    tb = {k: jnp.asarray(v) for k, v in host_tables().items()}
    count = sections.shape[0]
    nz, nx = lax.axis_size("gz"), lax.axis_size("xy")
    first = lax.axis_index("gz") * count
    target = jnp.arange(count, dtype=jnp.int32)[:, None] + skips
    live = ((skips > 0) & (first + target < count * nz)).astype(jnp.int32)
    own = forward_call(sections, tb)
    far = lax.ppermute(own[:REACH], "gz", [(i, (i - 1) % nz) for i in range(nz)])
    spec = jnp.concatenate([own, far], axis=0)
    flow, payload = pair_call(target, skips, live, patch_valid, velocity_start, spec, tb)
    displace = relax_call(step_size, mixing, payload, nz, nx)
    return flow, displace


def solution(mesh):
    in_specs = (
        P("gz", "xy", None),
        P("gz", None),
        P("gz", "xy", None),
        P("gz", None, "xy", None),
        P(),
        P(),
    )
    out_specs = (P("gz", None, None, "xy", None), P("gz", None, "xy", None))
    return jax.shard_map(body, mesh=mesh, in_specs=in_specs, out_specs=out_specs, check_vma=False)
```

```python
import functools
import jax
import jax.numpy as jnp
import numpy as np
import ml_dtypes
from jax import lax
from jax.experimental import pallas as pl
from jax.experimental.pallas import tpu as pltpu
from jax.sharding import PartitionSpec as P

PATCH = 64
HALF = 32
ITERS = 3
SHARP = 400.0
STIFF = 0.25
TINY = 1e-06
LOG2E = 1.4426950408889634
SCORE_EXP = SHARP / float(PATCH**4) * LOG2E
MESH = pl.DeviceIdType.MESH
STEPS = 11
NEAR, FAR = 2, 3


def host_tables():
    n = np.arange(PATCH)
    angle = ((n[:, None] * n[None, :]) % PATCH) * (2.0 * np.pi / PATCH)
    rounded = lambda a: np.where(np.abs(a) < 1e-9, 0.0, a).astype(ml_dtypes.bfloat16).astype(np.float64)
    cos, sin = rounded(np.cos(angle)), rounded(np.sin(angle))
    z = np.zeros((PATCH, PATCH))
    forward_cols = np.block([[cos, z, sin, z], [z, cos, z, sin]])
    forward_rows = np.concatenate([cos[:32], cos[32:33], sin[1:32]], axis=0)

    def couple(rr, ri, ir, ii):
        return np.block([[rr, z, ri, z], [z, rr, z, ri], [ir, z, ii, z], [z, ir, z, ii]])

    icols = couple(cos, sin, -sin, cos)
    rr, ri, ir, ii = (np.zeros((PATCH, PATCH)) for _ in range(4))
    rr[0] = cos[0]
    rr[1:32] = 2.0 * cos[1:32]
    ir[1:32] = -2.0 * sin[1:32]
    ir[0] = cos[32]
    ri[32] = cos[32]
    ri[33:] = 2.0 * cos[33:]
    ii[33:] = -2.0 * sin[33:]
    ii[32] = cos[0]
    ipack = couple(rr, ri, ir, ii)
    inverse_rows = np.zeros((64, 64))
    inverse_rows[:, 0] = 1.0
    inverse_rows[:, 1:32] = 2.0 * cos[:, 1:32]
    inverse_rows[:, 32] = cos[:, 32]
    inverse_rows[:, 33:] = -2.0 * sin[:, 1:32]
    last = np.concatenate([forward_rows, z, inverse_rows, z], axis=1)
    return np.concatenate([forward_cols, icols, ipack, last], axis=0).astype(ml_dtypes.bfloat16)


def half_sums(v, left):
    a = jnp.sum(jnp.where(left, v, 0.0), axis=1, keepdims=True)
    b = jnp.sum(jnp.where(left, 0.0, v), axis=1, keepdims=True)
    return jnp.where(left, a, b)


def tile_stats(x_ref, s, a, mean_ref, rs_ref, chunk=512):
    rows = pl.ds(pl.multiple_of(a * PATCH, PATCH), PATCH)
    left = lax.broadcasted_iota(jnp.int32, (1, 128), 1) < 64
    t = s * 2 + a
    scale = 1.0 / PATCH**2
    spans = range(0, chunk, 128)
    for c in range(0, x_ref.shape[2], chunk):
        x = x_ref[s, rows, c:c + chunk].astype(jnp.float32)
        total = jnp.sum(x, axis=0, keepdims=True)
        mean = jnp.concatenate([half_sums(total[:, k:k + 128], left) for k in spans], axis=1) * scale
        mean_ref[t, :, c:c + chunk] = mean
        d = x - mean
        total = jnp.sum(d * d, axis=0, keepdims=True)
        spread = jnp.concatenate([half_sums(total[:, k:k + 128], left) for k in spans], axis=1) * scale
        rs_ref[t, :, c:c + chunk] = lax.rsqrt(spread + 1e-5)


def tile_columns(x_ref, s, a, mean_ref, rs_ref, fcols, half_ref):
    rows = pl.ds(pl.multiple_of(a * PATCH, PATCH), PATCH)
    t = s * 2 + a
    for i in range(x_ref.shape[2] // 128):
        cols = slice(i * 128, (i + 1) * 128)
        x = x_ref[s, rows, cols].astype(jnp.float32)
        normed = ((x - mean_ref[t, :, cols]) * rs_ref[t, :, cols]).astype(jnp.bfloat16)
        half_ref[:, i * 256:(i + 1) * 256] = jnp.dot(normed, fcols, preferred_element_type=jnp.float32).astype(jnp.bfloat16)


def tile_rows(s, a, frows, half_ref, spec_ref):
    lane = lax.broadcasted_iota(jnp.int32, (8, 128), 1) % 64
    row0 = lax.broadcasted_iota(jnp.int32, (8, 128), 0) == 0
    upper = lane >= 32
    for i in range(spec_ref.shape[1]):
        both = jnp.dot(frows, half_ref[:, i * 256:(i + 1) * 256], preferred_element_type=jnp.float32)
        ca, cb = both[:HALF, :128], both[:HALF, 128:]
        sa, sb = both[HALF:, :128], both[HALF:, 128:]
        real, imag = ca - sb, sa + cb
        ca, cb, sa, sb = ca[:8], cb[:8], sa[:8], sb[:8]
        real0 = jnp.where(upper, sa, ca)
        imag0 = jnp.where(upper, sb, cb)
        imag0 = jnp.where(lane == 0, pltpu.roll(ca, 96, axis=1), jnp.where(lane == 32, pltpu.roll(sa, 32, axis=1), imag0))
        real = jnp.concatenate([jnp.where(row0, real0, real[:8]), real[8:]], axis=0)
        imag = jnp.concatenate([jnp.where(row0, imag0, imag[:8]), imag[8:]], axis=0)
        spec_ref[s * 2 + a, i] = jnp.concatenate([real, imag], axis=1).astype(jnp.bfloat16)


def pair_cross(tasks, count, icols, ipack, u_ref):
    lane = lax.broadcasted_iota(jnp.int32, (8, 128), 1) % 32
    row = lax.broadcasted_iota(jnp.int32, (8, 128), 0)
    special = (row == 0) & (lane == 0)
    blocks = []
    for mine_of, other_of in tasks:
        for i in range(count):
            mine, other = mine_of(i).astype(jnp.float32), other_of(i).astype(jnp.float32)
            r, m = mine[:, :128], mine[:, 128:]
            p, q = other[:, :128], other[:, 128:]
            rp, mq = r * p, m * q
            real, imag = rp + mq, m * p - r * q
            real = jnp.concatenate([jnp.where(special, rp[:8], real[:8]), real[8:]], axis=0)
            imag = jnp.concatenate([jnp.where(special, mq[:8], imag[:8]), imag[8:]], axis=0)
            blocks.append(jnp.concatenate([real, imag], axis=1).astype(jnp.bfloat16))
    n = len(blocks)
    inner = jnp.dot(jnp.concatenate(blocks, axis=0), icols, preferred_element_type=jnp.float32)
    first = jnp.dot(jnp.concatenate([b[:16] for b in blocks], axis=0), ipack, preferred_element_type=jnp.float32)
    row0 = lax.broadcasted_iota(jnp.int32, (8, 256), 0) == 0
    for i in range(n):
        head = jnp.where(row0, first[i * 16:i * 16 + 8], inner[i * 32:i * 32 + 8])
        u = jnp.concatenate([head, inner[i * 32 + 8:i * 32 + 32]], axis=0).astype(jnp.bfloat16)
        u_ref[:32, i * 128:(i + 1) * 128] = u[:, :128]
        u_ref[32:, i * 128:(i + 1) * 128] = u[:, 128:]


def pair_soft(u_ref, n, irows, m_ref, z_ref, r_ref, step):
    for h in range(0, n, 2):
        corr = jnp.dot(irows, u_ref[:, h * 128:(h + 2) * 128], preferred_element_type=jnp.float32)
        for i in (h, h + 1):
            e = [corr[8 * r:8 * r + 8, (i - h) * 128:(i - h + 1) * 128] for r in range(8)]
            m = functools.reduce(jnp.maximum, e)
            e = [jnp.exp2((v - m) * SCORE_EXP) for v in e]
            s3 = e[3]
            s2 = e[2] + s3
            s1 = e[1] + s2
            t4 = e[4]
            t5 = t4 + e[5]
            t6 = t5 + e[6]
            t7 = t6 + e[7]
            spot = pl.ds(pl.multiple_of((step * n + i) * 8, 8), 8)
            m_ref[spot] = m
            z_ref[spot] = (s1 + e[0]) + t7
            r_ref[spot] = ((s1 + s2) + s3) - ((t4 + t5) + (t6 + t7))


def pair_finish(m_ref, z_ref, r_ref, first, count):
    rows = count * 32
    lane = lax.broadcasted_iota(jnp.int32, (rows, 128), 1)
    left = lane < 64
    t2 = lane % 64
    shift = jnp.where(t2 < 32, t2, t2 - 64).astype(jnp.float32)
    pick = lambda ref, r: ref[pl.ds(first * 256 + r, rows, stride=8), :]
    top = functools.reduce(jnp.maximum, [pick(m_ref, r) for r in range(8)])
    a = jnp.max(jnp.where(left, top, -jnp.inf), axis=1, keepdims=True)
    b = jnp.max(jnp.where(left, -jnp.inf, top), axis=1, keepdims=True)
    peak = jnp.where(left, a, b)
    total = jnp.zeros((rows, 128), jnp.float32)
    along = jnp.zeros((rows, 128), jnp.float32)
    for r in range(8):
        w = jnp.exp2((pick(m_ref, r) - peak) * SCORE_EXP)
        z = pick(z_ref, r)
        total += w * z
        along += w * (8.0 * pick(r_ref, r) + float(r) * z)
    across = total * shift

    def sides(v):
        return (jnp.sum(jnp.where(left, v, 0.0), axis=1, keepdims=True), jnp.sum(jnp.where(left, 0.0, v), axis=1, keepdims=True))

    owner = lax.broadcasted_iota(jnp.int32, (rows, 128), 0) % 32
    mine = (lane % 64) // 2 == owner
    odd = lane % 2 == 1
    (tl, tr), (al, ar), (cl, cr) = sides(total), sides(along), sides(across)
    down = jnp.where(mine, jnp.where(odd, tr, tl), 0.0)
    up = jnp.where(mine, jnp.where(left, jnp.where(odd, ar, al), jnp.where(odd, cr, cl)), 0.0)
    fold = lambda v: [jnp.sum(v[k * 32:(k + 1) * 32], axis=0, keepdims=True) for k in range(count)]
    return [u / d for u, d in zip(fold(up), fold(down))]


def shifted(x, by):
    return pltpu.roll(x, (-by) % x.shape[0], axis=0)


def kernel(nz, nx, x_hbm, tab_hbm, skip_ref, step_ref, mix_ref, valid_ref, start_ref, flow_ref, out_ref,
           x_ref, tab_ref, mean_ref, rs_ref, half_ref, spec_ref, recv_ref, u_ref, m_ref, z_ref, r_ref,
           ext_ref, push_ref, back_ref, sent_ref, part1, part2,
           sem_x, sem_tab, sem_s, got_s, sem_e, got_e, sem_l, got_l, sem_b, got_b, sem_1, got_1, sem_2, got_2):
    gz = lax.axis_index("gz")
    xy = lax.axis_index("xy")
    groups = nz // 4
    yy, zc = gz // groups, gz % groups
    couples = spec_ref.shape[1]

    loads = [pltpu.make_async_copy(x_hbm.at[s], x_ref.at[s], sem_x.at[s]) for s in range(4)]
    for c in loads:
        c.start()
    tab_load = pltpu.make_async_copy(tab_hbm, tab_ref, sem_tab)
    tab_load.start()

    def at(db, dx):
        return (lax.rem(gz + db + nz, nz), lax.rem(xy + dx + nx, nx))

    def near(r):
        k = lax.rem(yy * nx + xy + r, 4 * nx)
        return (k // nx * groups + zc, lax.rem(k, nx))

    def along(r):
        return (yy * groups + lax.rem(zc + r, groups), xy)

    wide = [(db, dx) for db in range(-FAR, FAR + 1) for dx in (-1, 0, 1) if (db, dx) != (0, 0)]
    close = [(db, dx) for db, dx in wide if abs(db) <= NEAR]
    barrier = pltpu.get_barrier_semaphore()
    peers = [at(db, dx) for db, dx in wide] + [near(r) for r in range(1, 4 * nx)] + [along(r) for r in range(1, groups)]
    for peer in peers:
        pl.semaphore_signal(barrier, inc=1, device_id=peer, device_id_type=MESH)

    lanes = lax.broadcasted_iota(jnp.int32, (1, 128), 1)
    skip = [[skip_ref[s, j] for j in range(2)] for s in range(4)]
    live = [[(k > 0) & (gz * 4 + s + k < 4 * nz) for k in skip[s]] for s in range(4)]
    for s in range(4):
        ext_ref[1, NEAR, 0, s:s + 1, :] = jnp.concatenate(
            [start_ref[s, c, a:a + 1, :] for c in range(2) for a in range(2)], axis=1)
        row = jnp.concatenate([valid_ref[s, a:a + 1, :] for a in range(2)] * 2, axis=1).astype(jnp.float32)
        for d in (1, 2, 3):
            hit = ((skip[s][0] == d) & live[s][0]) | ((skip[s][1] == d) & live[s][1])
            row = jnp.where(lanes == 63 + d, jnp.where(hit, 1.0, 0.0), row)
        ext_ref[1, NEAR, 1, s:s + 1, :] = row

    def tile(i):
        return lax.rem((i + 1) // 2, 4), i % 2

    def stats(i):
        tile_stats(x_ref, *tile(i), mean_ref, rs_ref)

    def columns(i):
        tile_columns(x_ref, *tile(i), mean_ref, rs_ref, tab_ref[0:128], half_ref)

    def rows(i):
        tile_rows(*tile(i), tab_ref[640:704, 0:64], half_ref, spec_ref)

    def spectrum_copy(i):
        s, a = tile(i)
        slot = s + 2 * a
        return pltpu.make_async_remote_copy(
            src_ref=spec_ref.at[s * 2 + a], dst_ref=recv_ref.at[slot], send_sem=sem_s.at[slot], recv_sem=got_s.at[slot],
            device_id=(lax.rem(gz + nz - 1 + 2 * a, nz), xy), device_id_type=MESH)

    loads[0].wait()
    stats(0)
    loads[1].wait()
    stats(1)
    tab_load.wait()
    columns(0)
    loads[2].wait()
    loads[3].wait()
    pl.semaphore_wait(barrier, len(peers))
    early = []
    for n, (db, dx) in enumerate(close):
        early.append(pltpu.make_async_remote_copy(
            src_ref=ext_ref.at[1, NEAR], dst_ref=ext_ref.at[dx + 1, db + NEAR], send_sem=sem_e.at[n], recv_sem=got_e.at[n],
            device_id=at(-db, -dx), device_id_type=MESH))
        early[-1].start()

    def forward(i, _):
        rows(i - 2)
        columns(i - 1)
        stats(i)
        spectrum_copy(i - 2).start()
        return 0

    lax.fori_loop(2, 8, forward, 0)
    rows(6)
    columns(7)
    rows(7)

    def cross(tasks):
        pair_cross(tasks, couples, tab_ref[128:384], tab_ref[384:640], u_ref)

    def soft(step):
        pair_soft(u_ref, 2 * couples, tab_ref[640:704, 128:192], m_ref, z_ref, r_ref, step)

    def own(s, a):
        return lambda i: spec_ref[s * 2 + a, i]

    def got(slot):
        return lambda i: recv_ref[slot, i]

    def first_section(j):
        p = skip_ref[0, j]
        cross([(own(0, 0), own(p, 0)), (own(0, 1), own(p, 1))])

    def inside_block(i):
        s, p = i // 2, i - i // 4
        cross([(own(s, 0), own(p, 0)), (own(s, 1), own(p, 1))])

    def over_edge(k, m):
        cross([(own(k + 1, 0), got(m)), (got(3 + k), own(m, 1))])

    first_section(0)
    soft(0)
    first_section(1)

    def inside_step(i, _):
        soft(i - 1)
        inside_block(i)
        return 0

    lax.fori_loop(2, 5, inside_step, 0)
    for k in range(3):
        spectrum_copy(2 * k).wait_recv()
        spectrum_copy(2 * k + 1).wait_recv()
        base = 5 + k * (k + 1) // 2

        def edge_step(m, _, k=k, base=base):
            soft(base + m - 1)
            over_edge(k, m)
            return 0

        lax.fori_loop(0, k + 1, edge_step, 0)

    for c in early:
        c.wait()
    blocks = 2 * NEAR + 1
    size = 4 * blocks + 4
    here = slice(4 * NEAR, 4 * NEAR + 4)
    lane = lax.broadcasted_iota(jnp.int32, (size, 128), 1)
    col = lane % 32
    upper = (lane // 32) % 2 == 0
    inside = [jnp.where(xy > 0, 1.0, 0.0), 1.0, jnp.where(xy < nx - 1, 1.0, 0.0)]
    pad = jnp.zeros((4, 128), jnp.float32)
    weights, vel, valid_rows, live_rows = [], [], [], []
    for dx in range(3):
        info = jnp.concatenate([ext_ref[dx, k, 1] for k in range(blocks)] + [pad], axis=0)
        valid = jnp.where(lane < 64, info, pltpu.roll(info, 64, axis=1))
        on = [info[:, 64 + k:65 + k] for k in range(3)]
        weights.append([on[d - 1] * valid * shifted(valid, d) for d in (1, 2, 3)])
        vel.append(jnp.concatenate([ext_ref[dx, k, 0] for k in range(blocks)] + [pad], axis=0) * inside[dx])

    def force(fields, dx):
        v = fields[dx]
        above = fields[dx - 1] if dx > 0 else jnp.zeros_like(v)
        below = fields[dx + 1] if dx < 2 else jnp.zeros_like(v)
        lateral = jnp.where(col == 0, 0.0, pltpu.roll(v, 1, axis=1)) + jnp.where(col == 31, 0.0, pltpu.roll(v, 127, axis=1))
        down, up = pltpu.roll(v, 32, axis=1), pltpu.roll(v, 96, axis=1)
        vertical = jnp.where(upper, pltpu.roll(above, 96, axis=1) + up, down + pltpu.roll(below, 32, axis=1))
        out = STIFF * (lateral + vertical - 4.0 * v)
        for d in (1, 2, 3):
            pull = weights[dx][d - 1] * (shifted(v, d) - v)
            out += pull - shifted(pull, -d)
        return out * inside[dx]

    av = [force(vel, dx) for dx in range(3)]
    aav = force(av, 1)

    soft(STEPS - 1)
    flows = pair_finish(m_ref, z_ref, r_ref, 0, STEPS)

    for k in range(6):
        sent_ref[k:k + 1, :] = flows[5 + k]
    back = pltpu.make_async_remote_copy(
        src_ref=sent_ref, dst_ref=back_ref, send_sem=sem_b, recv_sem=got_b, device_id=at(-1, 0), device_id_type=MESH)
    back.start()

    low = (lanes // 32) % 2 == 0
    base = 4 * NEAR
    add = [[jnp.zeros((1, 128), jnp.float32) for _ in range(4)] for _ in range(3)]

    def spring(s, d):
        return weights[1][d - 1][base + s:base + s + 1]

    def push(source, target, value):
        for where, sign in ((source, -1.0), (target, 1.0)):
            add[1 + where // 4][where % 4] += sign * value

    for j in range(2):
        for d in (1, 2, 3):
            push(0, d, jnp.where(skip[0][j] == d, spring(0, d), 0.0) * flows[j])
    for i in (2, 3, 4):
        s, p = i // 2, i - i // 4
        push(s, p, spring(s, p - s) * flows[i])
    for k in range(3):
        for m in range(k + 1):
            f = flows[5 + k * (k + 1) // 2 + m]
            push(k + 1, 4 + m, jnp.where(low, spring(k + 1, 3 - k + m) * f, 0.0))
            push(k - 3, m, jnp.where(low, 0.0, spring(k - 3, 3 - k + m) * f))
    for k in range(3):
        push_ref[1, FAR, k] = jnp.concatenate(add[k], axis=0)
    late = []
    for n, (db, dx) in enumerate(wide):
        late.append(pltpu.make_async_remote_copy(
            src_ref=push_ref.at[1, FAR], dst_ref=push_ref.at[dx + 1, db + FAR], send_sem=sem_l.at[n], recv_sem=got_l.at[n],
            device_id=at(-db, -dx), device_id_type=MESH))
        late[-1].start()
    for c in late:
        c.wait_recv()
    bias = []
    for dx in range(3):
        parts = [push_ref[dx, k + 1, 1] + push_ref[dx, k, 2] + push_ref[dx, k + 2, 0] for k in range(blocks)]
        bias.append(jnp.concatenate(parts + [pad], axis=0) * inside[dx])
    ab = [force(bias, dx) for dx in range(3)]
    aab = force(ab, 1)
    basis = [x[here] for x in (vel[1], bias[1], av[1], ab[1], aav, aab)]

    index, sums = {}, []
    for i in range(6):
        for j in range(i, 6):
            index[i, j] = index[j, i] = len(sums)
            sums.append(jnp.sum(basis[i] * basis[j], axis=0, keepdims=True))
    sums = jnp.sum(jnp.concatenate(sums + [jnp.zeros((3, 128), jnp.float32)], axis=0), axis=1, keepdims=True)
    diagonal = lax.broadcasted_iota(jnp.int32, (24, 128), 0) == lax.broadcasted_iota(jnp.int32, (24, 128), 1)
    part1[0] = jnp.sum(jnp.where(diagonal, sums, 0.0), axis=0, keepdims=True)

    def scatter(part, count, peer, sem, got):
        sends = []
        for r in range(1, count):
            sends.append(pltpu.make_async_remote_copy(
                src_ref=part.at[0], dst_ref=part.at[r], send_sem=sem.at[r], recv_sem=got.at[r],
                device_id=peer(r), device_id_type=MESH))
            sends[-1].start()
        return sends

    def collect(part, sends):
        for c in sends:
            c.wait_recv()
        return functools.reduce(jnp.add, [part[r] for r in range(len(sends) + 1)])

    sends1 = scatter(part1, 4 * nx, near, sem_1, got_1)

    back.wait_recv()
    full = flows[:5] + [jnp.where(low, flows[5 + k], back_ref[k:k + 1, :]) for k in range(6)]
    step_of = {(1, 1): 2, (1, 2): 3, (2, 1): 4, (1, 3): 5, (2, 2): 6, (2, 3): 7, (3, 1): 8, (3, 2): 9, (3, 3): 10}
    for s in range(4):
        for j in range(2):
            if s == 0:
                f = full[j]
            else:
                f = jnp.where(skip[s][j] == 1, full[step_of[s, 1]], jnp.where(skip[s][j] == 2, full[step_of[s, 2]], full[step_of[s, 3]]))
            f = jnp.where(live[s][j], f, 0.0)
            for c in range(2):
                for a in range(2):
                    flow_ref[s, j, c, a:a + 1, :] = f[:, c * 64 + a * 32:c * 64 + a * 32 + 32]

    part2[0] = collect(part1, sends1)
    sends2 = scatter(part2, groups, along, sem_2, got_2)
    gram = collect(part2, sends2)
    g = {k: jnp.broadcast_to(gram[:, n:n + 1], (1, 128)) for k, n in index.items()}

    def dot(p, q):
        terms = [p[i] * q[j] * g[i, j] for i in range(6) for j in range(6) if p[i] is not None and q[j] is not None]
        return functools.reduce(jnp.add, terms)

    def plus(*xs):
        xs = [x for x in xs if x is not None]
        return functools.reduce(jnp.add, xs) if xs else None

    def times(k, x):
        return None if x is None else k * x

    one = jnp.ones((1, 128), jnp.float32)
    v = [one] + [None] * 5
    d = [None] * 6
    for it in range(ITERS):
        f = [None, one] + d[:4]
        power, speed, strength = dot(f, v), dot(v, v), dot(f, f)
        speed, strength = jnp.maximum(speed, 0.0), jnp.maximum(strength, 0.0)
        gating = 0.5 + 0.5 * power / jnp.sqrt((speed + TINY) * (strength + TINY))
        ratio = jnp.sqrt((speed + TINY) / (strength + TINY))
        mix, step = mix_ref[it], step_ref[it]
        kv, kf = gating * (1.0 - mix), gating * (mix * ratio) + step
        v = [plus(times(kv, v[i]), times(kf, f[i])) for i in range(6)]
        d = [plus(d[i], times(step, v[i])) for i in range(6)]
    result = functools.reduce(jnp.add, [d[i] * basis[i] for i in range(6)])
    for c in range(2):
        for a in range(2):
            spot = c * 64 + a * 32
            for s in range(4):
                out_ref[s, c, a:a + 1, :] = result[s:s + 1, spot:spot + 32]

    for i in range(6):
        spectrum_copy(i).wait_send()
    for c in late + [back] + sends1 + sends2:
        c.wait_send()


def body(sections, skips, patch_valid, velocity_start, step_size, mixing):
    nz, nx = lax.axis_size("gz"), lax.axis_size("xy")
    vm, sm, hbm = (pl.BlockSpec(memory_space=k) for k in (pltpu.VMEM, pltpu.SMEM, pl.ANY))
    tables = jnp.asarray(host_tables())
    width = sections.shape[2]
    couples = width // 128
    dma = pltpu.SemaphoreType.DMA
    wide = 3 * (2 * FAR + 1) - 1
    close = 3 * (2 * NEAR + 1) - 1
    f32, bf16 = jnp.float32, jnp.bfloat16
    vmem = pltpu.VMEM
    return pl.pallas_call(
        functools.partial(kernel, nz, nx),
        out_shape=(jax.ShapeDtypeStruct((4, 2, 2, 2, 32), f32), jax.ShapeDtypeStruct((4, 2, 2, 32), f32)),
        in_specs=[hbm, hbm, sm, sm, sm, vm, vm], out_specs=(vm, vm),
        scratch_shapes=[
            vmem(sections.shape, bf16), vmem(tables.shape, bf16),
            vmem((8, 1, width), f32), vmem((8, 1, width), f32),
            vmem((64, couples * 256), bf16),
            vmem((8, couples, HALF, 256), bf16), vmem((6, couples, HALF, 256), bf16),
            vmem((64, couples * 256), bf16),
            vmem((STEPS * couples * 16, 128), f32), vmem((STEPS * couples * 16, 128), f32), vmem((STEPS * couples * 16, 128), f32),
            vmem((3, 2 * NEAR + 1, 2, 4, 128), f32), vmem((3, 2 * FAR + 1, 3, 4, 128), f32),
            vmem((6, 128), f32), vmem((6, 128), f32),
            vmem((4 * nx, 1, 128), f32), vmem((nz // 4, 1, 128), f32),
            dma((4,)), dma, dma((6,)), dma((6,)), dma((close,)), dma((close,)), dma((wide,)), dma((wide,)), dma, dma,
            dma((4 * nx,)), dma((4 * nx,)), dma((nz // 4,)), dma((nz // 4,)),
        ],
        compiler_params=pltpu.CompilerParams(collective_id=0, has_side_effects=True, vmem_limit_bytes=56 * 2**20),
        name="flow_relax",
    )(sections, tables, skips, step_size, mixing, patch_valid, velocity_start)


def solution(mesh):
    in_specs = (
        P("gz", "xy", None),
        P("gz", None),
        P("gz", "xy", None),
        P("gz", None, "xy", None),
        P(),
        P(),
    )
    out_specs = (P("gz", None, None, "xy", None), P("gz", None, "xy", None))
    return jax.shard_map(body, mesh=mesh, in_specs=in_specs, out_specs=out_specs, check_vma=False)
```

```python
import functools
import jax
import jax.numpy as jnp
import numpy as np
import ml_dtypes
from jax import lax
from jax.experimental import pallas as pl
from jax.experimental.pallas import tpu as pltpu
from jax.sharding import PartitionSpec as P

PATCH = 64
HALF = 32
ITERS = 3
SHARP = 400.0
STIFF = 0.25
TINY = 1e-06
LOG2E = 1.4426950408889634
SCORE_EXP = SHARP / float(PATCH**4) * LOG2E
MESH = pl.DeviceIdType.MESH
STEPS = 11
NEAR, FAR = 2, 3


def host_tables():
    n = np.arange(PATCH)
    angle = ((n[:, None] * n[None, :]) % PATCH) * (2.0 * np.pi / PATCH)
    rounded = lambda a: np.where(np.abs(a) < 1e-9, 0.0, a).astype(ml_dtypes.bfloat16).astype(np.float64)
    cos, sin = rounded(np.cos(angle)), rounded(np.sin(angle))
    z = np.zeros((PATCH, PATCH))
    forward_cols = np.block([[cos, z, sin, z], [z, cos, z, sin]])
    forward_rows = np.concatenate([cos[:32], cos[32:33], sin[1:32]], axis=0)

    def couple(rr, ri, ir, ii):
        return np.block([[rr, z, ri, z], [z, rr, z, ri], [ir, z, ii, z], [z, ir, z, ii]])

    icols = couple(cos, sin, -sin, cos)
    rr, ri, ir, ii = (np.zeros((PATCH, PATCH)) for _ in range(4))
    rr[0] = cos[0]
    rr[1:32] = 2.0 * cos[1:32]
    ir[1:32] = -2.0 * sin[1:32]
    ir[0] = cos[32]
    ri[32] = cos[32]
    ri[33:] = 2.0 * cos[33:]
    ii[33:] = -2.0 * sin[33:]
    ii[32] = cos[0]
    ipack = couple(rr, ri, ir, ii)
    inverse_rows = np.zeros((64, 64))
    inverse_rows[:, 0] = 1.0
    inverse_rows[:, 1:32] = 2.0 * cos[:, 1:32]
    inverse_rows[:, 32] = cos[:, 32]
    inverse_rows[:, 33:] = -2.0 * sin[:, 1:32]
    last = np.concatenate([forward_rows, z, inverse_rows, z], axis=1)
    return np.concatenate([forward_cols, icols, ipack, last], axis=0).astype(ml_dtypes.bfloat16)


def half_sums(v, left):
    a = jnp.sum(jnp.where(left, v, 0.0), axis=1, keepdims=True)
    b = jnp.sum(jnp.where(left, 0.0, v), axis=1, keepdims=True)
    return jnp.where(left, a, b)


def tile_stats(x_ref, s, a, mean_ref, rs_ref, chunk=512):
    rows = pl.ds(pl.multiple_of(a * PATCH, PATCH), PATCH)
    left = lax.broadcasted_iota(jnp.int32, (1, 128), 1) < 64
    t = s * 2 + a
    scale = 1.0 / PATCH**2
    spans = range(0, chunk, 128)
    for c in range(0, x_ref.shape[2], chunk):
        x = x_ref[s, rows, c:c + chunk].astype(jnp.float32)
        total = jnp.sum(x, axis=0, keepdims=True)
        mean = jnp.concatenate([half_sums(total[:, k:k + 128], left) for k in spans], axis=1) * scale
        mean_ref[t, :, c:c + chunk] = mean
        d = x - mean
        total = jnp.sum(d * d, axis=0, keepdims=True)
        spread = jnp.concatenate([half_sums(total[:, k:k + 128], left) for k in spans], axis=1) * scale
        rs_ref[t, :, c:c + chunk] = lax.rsqrt(spread + 1e-5)


def tile_columns(x_ref, s, a, mean_ref, rs_ref, fcols, half_ref):
    rows = pl.ds(pl.multiple_of(a * PATCH, PATCH), PATCH)
    t = s * 2 + a
    for i in range(x_ref.shape[2] // 128):
        cols = slice(i * 128, (i + 1) * 128)
        x = x_ref[s, rows, cols].astype(jnp.float32)
        normed = ((x - mean_ref[t, :, cols]) * rs_ref[t, :, cols]).astype(jnp.bfloat16)
        half_ref[:, i * 256:(i + 1) * 256] = jnp.dot(normed, fcols, preferred_element_type=jnp.float32).astype(jnp.bfloat16)


def tile_rows(s, a, frows, half_ref, spec_ref):
    lane = lax.broadcasted_iota(jnp.int32, (8, 128), 1) % 64
    row0 = lax.broadcasted_iota(jnp.int32, (8, 128), 0) == 0
    upper = lane >= 32
    for i in range(spec_ref.shape[1]):
        both = jnp.dot(frows, half_ref[:, i * 256:(i + 1) * 256], preferred_element_type=jnp.float32)
        ca, cb = both[:HALF, :128], both[:HALF, 128:]
        sa, sb = both[HALF:, :128], both[HALF:, 128:]
        real, imag = ca - sb, sa + cb
        ca, cb, sa, sb = ca[:8], cb[:8], sa[:8], sb[:8]
        real0 = jnp.where(upper, sa, ca)
        imag0 = jnp.where(upper, sb, cb)
        imag0 = jnp.where(lane == 0, pltpu.roll(ca, 96, axis=1), jnp.where(lane == 32, pltpu.roll(sa, 32, axis=1), imag0))
        real = jnp.concatenate([jnp.where(row0, real0, real[:8]), real[8:]], axis=0)
        imag = jnp.concatenate([jnp.where(row0, imag0, imag[:8]), imag[8:]], axis=0)
        spec_ref[s * 2 + a, i] = jnp.concatenate([real, imag], axis=1).astype(jnp.bfloat16)


def pair_cross(tasks, count, icols, ipack, u_ref):
    lane = lax.broadcasted_iota(jnp.int32, (8, 128), 1) % 32
    row = lax.broadcasted_iota(jnp.int32, (8, 128), 0)
    special = (row == 0) & (lane == 0)
    blocks = []
    for mine_of, other_of in tasks:
        for i in range(count):
            mine, other = mine_of(i).astype(jnp.float32), other_of(i).astype(jnp.float32)
            r, m = mine[:, :128], mine[:, 128:]
            p, q = other[:, :128], other[:, 128:]
            rp, mq = r * p, m * q
            real, imag = rp + mq, m * p - r * q
            real = jnp.concatenate([jnp.where(special, rp[:8], real[:8]), real[8:]], axis=0)
            imag = jnp.concatenate([jnp.where(special, mq[:8], imag[:8]), imag[8:]], axis=0)
            blocks.append(jnp.concatenate([real, imag], axis=1).astype(jnp.bfloat16))
    n = len(blocks)
    inner = jnp.dot(jnp.concatenate(blocks, axis=0), icols, preferred_element_type=jnp.float32)
    first = jnp.dot(jnp.concatenate([b[:16] for b in blocks], axis=0), ipack, preferred_element_type=jnp.float32)
    row0 = lax.broadcasted_iota(jnp.int32, (8, 256), 0) == 0
    for i in range(n):
        head = jnp.where(row0, first[i * 16:i * 16 + 8], inner[i * 32:i * 32 + 8])
        u = jnp.concatenate([head, inner[i * 32 + 8:i * 32 + 32]], axis=0).astype(jnp.bfloat16)
        u_ref[:32, i * 128:(i + 1) * 128] = u[:, :128]
        u_ref[32:, i * 128:(i + 1) * 128] = u[:, 128:]


def pair_soft(u_ref, n, irows, m_ref, z_ref, r_ref, step):
    for h in range(0, n, 2):
        corr = jnp.dot(irows, u_ref[:, h * 128:(h + 2) * 128], preferred_element_type=jnp.float32)
        for i in (h, h + 1):
            e = [corr[8 * r:8 * r + 8, (i - h) * 128:(i - h + 1) * 128] for r in range(8)]
            m = functools.reduce(jnp.maximum, e)
            e = [jnp.exp2((v - m) * SCORE_EXP) for v in e]
            s3 = e[3]
            s2 = e[2] + s3
            s1 = e[1] + s2
            t4 = e[4]
            t5 = t4 + e[5]
            t6 = t5 + e[6]
            t7 = t6 + e[7]
            spot = pl.ds(pl.multiple_of((step * n + i) * 8, 8), 8)
            m_ref[spot] = m
            z_ref[spot] = (s1 + e[0]) + t7
            r_ref[spot] = ((s1 + s2) + s3) - ((t4 + t5) + (t6 + t7))


def pair_finish(m_ref, z_ref, r_ref, first, count):
    rows = count * 32
    lane = lax.broadcasted_iota(jnp.int32, (rows, 128), 1)
    left = lane < 64
    t2 = lane % 64
    shift = jnp.where(t2 < 32, t2, t2 - 64).astype(jnp.float32)
    pick = lambda ref, r: ref[pl.ds(first * 256 + r, rows, stride=8), :]
    top = functools.reduce(jnp.maximum, [pick(m_ref, r) for r in range(8)])
    a = jnp.max(jnp.where(left, top, -jnp.inf), axis=1, keepdims=True)
    b = jnp.max(jnp.where(left, -jnp.inf, top), axis=1, keepdims=True)
    peak = jnp.where(left, a, b)
    total = jnp.zeros((rows, 128), jnp.float32)
    along = jnp.zeros((rows, 128), jnp.float32)
    for r in range(8):
        w = jnp.exp2((pick(m_ref, r) - peak) * SCORE_EXP)
        z = pick(z_ref, r)
        total += w * z
        along += w * (8.0 * pick(r_ref, r) + float(r) * z)
    across = total * shift

    def sides(v):
        return (jnp.sum(jnp.where(left, v, 0.0), axis=1, keepdims=True), jnp.sum(jnp.where(left, 0.0, v), axis=1, keepdims=True))

    owner = lax.broadcasted_iota(jnp.int32, (rows, 128), 0) % 32
    mine = (lane % 64) // 2 == owner
    odd = lane % 2 == 1
    (tl, tr), (al, ar), (cl, cr) = sides(total), sides(along), sides(across)
    down = jnp.where(mine, jnp.where(odd, tr, tl), 0.0)
    up = jnp.where(mine, jnp.where(left, jnp.where(odd, ar, al), jnp.where(odd, cr, cl)), 0.0)
    fold = lambda v: [jnp.sum(v[k * 32:(k + 1) * 32], axis=0, keepdims=True) for k in range(count)]
    return [u / d for u, d in zip(fold(up), fold(down))]


def halo(reach):
    return [(db, dx) for dx in (0, -1, 1) for db in range(-reach, reach + 1)
            if (db, dx) != (0, 0) and abs(db) + abs(dx) <= reach]


def shifted(x, by):
    return pltpu.roll(x, (-by) % x.shape[0], axis=0)


def edge_base(k):
    return 5 + 3 * k - k * (k - 1) // 2


def kernel(nz, nx, x_hbm, tab_hbm, skip_ref, step_ref, mix_ref, valid_ref, start_ref, out_ref,
           x_ref, tab_ref, mean_ref, rs_ref, half_ref, spec_ref, recv_ref, u_ref, m_ref, z_ref, r_ref,
           ext_ref, push_ref, back_ref, sent_ref, part1, part2,
           sem_x, sem_tab, sem_s, got_s, sem_e, got_e, sem_l, got_l, sem_b, got_b, sem_1, got_1, sem_2, got_2):
    gz = lax.axis_index("gz")
    xy = lax.axis_index("xy")
    groups = nz // 4
    yy, zc = gz // groups, gz % groups
    couples = spec_ref.shape[1]

    def tile(i):
        half = i // 2
        return half + i % 2 * (3 - 2 * half), i % 2

    def tile_load(i):
        s, a = tile(i)
        part = pl.ds(a * PATCH, PATCH)
        return pltpu.make_async_copy(x_hbm.at[s, part], x_ref.at[s, part], sem_x.at[i])

    loads = [tile_load(i) for i in range(8)]
    for c in loads:
        c.start()
    tab_load = pltpu.make_async_copy(tab_hbm, tab_ref, sem_tab)
    tab_load.start()

    def at(db, dx):
        return (lax.rem(gz + db + nz, nz), lax.rem(xy + dx + nx, nx))

    def near(r):
        k = lax.rem(yy * nx + xy + r, 4 * nx)
        return (k // nx * groups + zc, lax.rem(k, nx))

    def along(r):
        return (yy * groups + lax.rem(zc + r, groups), xy)

    wide, close = halo(FAR), halo(NEAR)
    barrier = pltpu.get_barrier_semaphore()
    peers = [at(db, dx) for db, dx in wide] + [near(r) for r in range(1, 4 * nx)] + [along(r) for r in range(1, groups)]
    for peer in peers:
        pl.semaphore_signal(barrier, inc=1, device_id=peer, device_id_type=MESH)

    lanes = lax.broadcasted_iota(jnp.int32, (1, 128), 1)
    skip = [[skip_ref[j, s] for j in range(2)] for s in range(4)]
    live = [[(k > 0) & (gz * 4 + s + k < 4 * nz) for k in skip[s]] for s in range(4)]
    for s in range(4):
        ext_ref[1, NEAR, 0, s:s + 1, :] = jnp.concatenate(
            [start_ref[s, c, a:a + 1, :] for c in range(2) for a in range(2)], axis=1)
        row = jnp.concatenate([valid_ref[s, a:a + 1, :] for a in range(2)] * 2, axis=1).astype(jnp.float32)
        for d in (1, 2, 3):
            hit = ((skip[s][0] == d) & live[s][0]) | ((skip[s][1] == d) & live[s][1])
            row = jnp.where(lanes == 63 + d, jnp.where(hit, 1.0, 0.0), row)
        ext_ref[1, NEAR, 1, s:s + 1, :] = row

    def stats(i):
        tile_stats(x_ref, *tile(i), mean_ref, rs_ref)

    def columns(i):
        tile_columns(x_ref, *tile(i), mean_ref, rs_ref, tab_ref[0:128], half_ref)

    def rows(i):
        tile_rows(*tile(i), tab_ref[640:704, 0:64], half_ref, spec_ref)

    def spectrum_copy(i):
        s, a = tile(i)
        slot = s + 2 * a
        return pltpu.make_async_remote_copy(
            src_ref=spec_ref.at[s * 2 + a], dst_ref=recv_ref.at[slot], send_sem=sem_s.at[slot], recv_sem=got_s.at[slot],
            device_id=(lax.rem(gz + nz - 1 + 2 * a, nz), xy), device_id_type=MESH)

    loads[0].wait()
    stats(0)
    loads[1].wait()
    stats(1)
    tab_load.wait()
    columns(0)
    for c in loads[2:]:
        c.wait()
    pl.semaphore_wait(barrier, len(peers))
    early = []
    for n, (db, dx) in enumerate(close):
        early.append(pltpu.make_async_remote_copy(
            src_ref=ext_ref.at[1, NEAR], dst_ref=ext_ref.at[dx + 1, db + NEAR], send_sem=sem_e.at[n], recv_sem=got_e.at[n],
            device_id=at(-db, -dx), device_id_type=MESH))
        early[-1].start()

    def forward(i, _):
        rows(i - 2)
        columns(i - 1)
        stats(i)
        spectrum_copy(i - 2).start()
        return 0

    lax.fori_loop(2, 8, forward, 0)
    rows(6)
    columns(7)
    rows(7)

    def cross(tasks):
        pair_cross(tasks, couples, tab_ref[128:384], tab_ref[384:640], u_ref)

    def soft(step):
        pair_soft(u_ref, 2 * couples, tab_ref[640:704, 128:192], m_ref, z_ref, r_ref, step)

    def own(s, a):
        return lambda i: spec_ref[s * 2 + a, i]

    def got(slot):
        return lambda i: recv_ref[slot, i]

    def first_section(j):
        p = skip_ref[j, 0]
        cross([(own(0, 0), own(p, 0)), (own(0, 1), own(p, 1))])

    def inside_block(i):
        s, p = i // 2, i - i // 4
        cross([(own(s, 0), own(p, 0)), (own(s, 1), own(p, 1))])

    def over_edge(k, q):
        cross([(own(k + 1 + q, 0), got(k)), (got(5 - k), own(q, 1))])

    first_section(0)
    soft(0)
    first_section(1)

    def inside_step(i, _):
        soft(i - 1)
        inside_block(i)
        return 0

    lax.fori_loop(2, 5, inside_step, 0)
    for k in range(3):
        spectrum_copy(2 * k).wait_recv()
        spectrum_copy(2 * k + 1).wait_recv()

        def edge_step(q, _, k=k):
            soft(edge_base(k) + q - 1)
            over_edge(k, q)
            return 0

        lax.fori_loop(0, 3 - k, edge_step, 0)

    for c in early:
        c.wait_recv()
    blocks = 2 * NEAR + 1
    size = 4 * blocks + 4
    here = slice(4 * NEAR, 4 * NEAR + 4)
    lane = lax.broadcasted_iota(jnp.int32, (size, 128), 1)
    col = lane % 32
    upper = (lane // 32) % 2 == 0
    inside = [jnp.where(xy > 0, 1.0, 0.0), 1.0, jnp.where(xy < nx - 1, 1.0, 0.0)]
    pad = jnp.zeros((4, 128), jnp.float32)

    def reaches(dx, k):
        return abs(k - NEAR) + abs(dx - 1) <= NEAR

    def gather(dx, f):
        return jnp.concatenate([ext_ref[dx, k, f] if reaches(dx, k) else pad for k in range(blocks)] + [pad], axis=0)

    def springs(dx):
        info = gather(dx, 1)
        valid = jnp.where(lane < 64, info, pltpu.roll(info, 64, axis=1))
        return [info[:, 63 + d:64 + d] * valid * shifted(valid, d) for d in (1, 2, 3)]

    weights = [None, springs(1), None]
    soft(STEPS - 1)
    flows = pair_finish(m_ref, z_ref, r_ref, 0, STEPS)

    for k in range(6):
        sent_ref[k:k + 1, :] = flows[5 + k]
    back = pltpu.make_async_remote_copy(
        src_ref=sent_ref, dst_ref=back_ref, send_sem=sem_b, recv_sem=got_b, device_id=at(-1, 0), device_id_type=MESH)
    back.start()

    low = (lanes // 32) % 2 == 0
    base = 4 * NEAR
    add = [[jnp.zeros((1, 128), jnp.float32) for _ in range(4)] for _ in range(3)]

    def spring(s, d):
        return weights[1][d - 1][base + s:base + s + 1]

    def push(source, target, value):
        for where, sign in ((source, -1.0), (target, 1.0)):
            add[1 + where // 4][where % 4] += sign * value

    for j in range(2):
        for d in (1, 2, 3):
            push(0, d, jnp.where(skip[0][j] == d, spring(0, d), 0.0) * flows[j])
    for i in (2, 3, 4):
        s, p = i // 2, i - i // 4
        push(s, p, spring(s, p - s) * flows[i])
    for k in range(3):
        for q in range(3 - k):
            f = flows[edge_base(k) + q]
            push(k + 1 + q, 4 + k, jnp.where(low, spring(k + 1 + q, 3 - q) * f, 0.0))
            push(-1 - k, q, jnp.where(low, 0.0, spring(-1 - k, 1 + k + q) * f))
    for k in range(3):
        push_ref[1, FAR, k] = jnp.concatenate(add[k], axis=0)
    late = []
    for n, (db, dx) in enumerate(wide):
        late.append(pltpu.make_async_remote_copy(
            src_ref=push_ref.at[1, FAR], dst_ref=push_ref.at[dx + 1, db + FAR], send_sem=sem_l.at[n], recv_sem=got_l.at[n],
            device_id=at(-db, -dx), device_id_type=MESH))
        late[-1].start()

    weights = [springs(0), weights[1], springs(2)]
    vel = [gather(dx, 0) * inside[dx] for dx in range(3)]

    def force(fields, dx):
        v = fields[dx]
        above = fields[dx - 1] if dx > 0 else jnp.zeros_like(v)
        below = fields[dx + 1] if dx < 2 else jnp.zeros_like(v)
        lateral = jnp.where(col == 0, 0.0, pltpu.roll(v, 1, axis=1)) + jnp.where(col == 31, 0.0, pltpu.roll(v, 127, axis=1))
        down, up = pltpu.roll(v, 32, axis=1), pltpu.roll(v, 96, axis=1)
        vertical = jnp.where(upper, pltpu.roll(above, 96, axis=1) + up, down + pltpu.roll(below, 32, axis=1))
        out = STIFF * (lateral + vertical - 4.0 * v)
        for d in (1, 2, 3):
            pull = weights[dx][d - 1] * (shifted(v, d) - v)
            out += pull - shifted(pull, -d)
        return out * inside[dx]

    av = [force(vel, dx) for dx in range(3)]
    aav = force(av, 1)
    for c in late:
        c.wait_recv()
    bias = []
    for dx in range(3):
        parts = [push_ref[dx, k + 1, 1] + push_ref[dx, k, 2] + push_ref[dx, k + 2, 0] if reaches(dx, k) else pad
                 for k in range(blocks)]
        bias.append(jnp.concatenate(parts + [pad], axis=0) * inside[dx])
    ab = [force(bias, dx) for dx in range(3)]
    aab = force(ab, 1)
    basis = [x[here] for x in (vel[1], bias[1], av[1], ab[1], aav, aab)]

    index, sums = {}, []
    for i in range(6):
        for j in range(i, 6):
            index[i, j] = index[j, i] = len(sums)
            sums.append(jnp.sum(basis[i] * basis[j], axis=0, keepdims=True))
    sums = jnp.sum(jnp.concatenate(sums + [jnp.zeros((3, 128), jnp.float32)], axis=0), axis=1, keepdims=True)
    diagonal = lax.broadcasted_iota(jnp.int32, (24, 128), 0) == lax.broadcasted_iota(jnp.int32, (24, 128), 1)
    part1[0] = jnp.sum(jnp.where(diagonal, sums, 0.0), axis=0, keepdims=True)

    def scatter(part, count, peer, sem, got):
        sends = []
        for r in range(1, count):
            sends.append(pltpu.make_async_remote_copy(
                src_ref=part.at[0], dst_ref=part.at[r], send_sem=sem.at[r], recv_sem=got.at[r],
                device_id=peer(r), device_id_type=MESH))
            sends[-1].start()
        return sends

    def collect(part, sends):
        for c in sends:
            c.wait_recv()
        return functools.reduce(jnp.add, [part[r] for r in range(len(sends) + 1)])

    sends1 = scatter(part1, 4 * nx, near, sem_1, got_1)

    back.wait_recv()

    def flow_at(s, d):
        if s + d < 4:
            return flows[2 * s - 1 + d if s == 1 else 4]
        far = flows[edge_base(s + d - 4) + 3 - d]
        row = edge_base(3 - s) + s + d - 4 - 5
        return jnp.where(low, far, back_ref[row:row + 1, :])

    for s in range(4):
        for j in range(2):
            if s == 0:
                f = flows[j]
            else:
                f = flow_at(s, 3)
                for d in (1, 2):
                    f = jnp.where(skip[s][j] == d, flow_at(s, d), f)
            out_ref[2 * s + j:2 * s + j + 1, :] = jnp.where(live[s][j], f, 0.0)

    part2[0] = collect(part1, sends1)
    sends2 = scatter(part2, groups, along, sem_2, got_2)
    gram = collect(part2, sends2)
    g = {k: jnp.broadcast_to(gram[:, n:n + 1], (1, 128)) for k, n in index.items()}

    def dot(p, q):
        terms = [p[i] * q[j] * g[i, j] for i in range(6) for j in range(6) if p[i] is not None and q[j] is not None]
        return functools.reduce(jnp.add, terms)

    def plus(*xs):
        xs = [x for x in xs if x is not None]
        return functools.reduce(jnp.add, xs) if xs else None

    def times(k, x):
        return None if x is None else k * x

    one = jnp.ones((1, 128), jnp.float32)
    v = [one] + [None] * 5
    d = [None] * 6
    for it in range(ITERS):
        f = [None, one] + d[:4]
        power, speed, strength = dot(f, v), dot(v, v), dot(f, f)
        speed, strength = jnp.maximum(speed, 0.0), jnp.maximum(strength, 0.0)
        gating = 0.5 + 0.5 * power / jnp.sqrt((speed + TINY) * (strength + TINY))
        ratio = jnp.sqrt((speed + TINY) / (strength + TINY))
        mix, step = mix_ref[it], step_ref[it]
        kv, kf = gating * (1.0 - mix), gating * (mix * ratio) + step
        v = [plus(times(kv, v[i]), times(kf, f[i])) for i in range(6)]
        d = [plus(d[i], times(step, v[i])) for i in range(6)]
    result = functools.reduce(jnp.add, [d[i] * basis[i] for i in range(6)])
    out_ref[8:12, :] = result

    for i in range(6):
        spectrum_copy(i).wait_send()
    for c in early + late + [back] + sends1 + sends2:
        c.wait_send()


def unpack_kernel(packed_ref, flow_ref, displace_ref):
    for c in range(2):
        for a in range(2):
            lanes = slice(c * 64 + a * 32, c * 64 + a * 32 + 32)
            for s in range(4):
                displace_ref[s, c, a:a + 1, :] = packed_ref[8 + s:9 + s, lanes]
                for j in range(2):
                    flow_ref[s, j, c, a:a + 1, :] = packed_ref[2 * s + j:2 * s + j + 1, lanes]


def body(sections, skips, patch_valid, velocity_start, step_size, mixing):
    nz, nx = lax.axis_size("gz"), lax.axis_size("xy")
    vm, sm, hbm = (pl.BlockSpec(memory_space=k) for k in (pltpu.VMEM, pltpu.SMEM, pl.ANY))
    tables = jnp.asarray(host_tables())
    width = sections.shape[2]
    couples = width // 128
    dma = pltpu.SemaphoreType.DMA
    wide, close = len(halo(FAR)), len(halo(NEAR))
    f32, bf16 = jnp.float32, jnp.bfloat16
    vmem = pltpu.VMEM
    packed = pl.pallas_call(
        functools.partial(kernel, nz, nx),
        out_shape=jax.ShapeDtypeStruct((12, 128), f32),
        in_specs=[hbm, hbm, sm, sm, sm, vm, vm], out_specs=vm,
        scratch_shapes=[
            vmem(sections.shape, bf16), vmem(tables.shape, bf16),
            vmem((8, 1, width), f32), vmem((8, 1, width), f32),
            vmem((64, couples * 256), bf16),
            vmem((8, couples, HALF, 256), bf16), vmem((6, couples, HALF, 256), bf16),
            vmem((64, couples * 256), bf16),
            vmem((STEPS * couples * 16, 128), f32), vmem((STEPS * couples * 16, 128), f32), vmem((STEPS * couples * 16, 128), f32),
            vmem((3, 2 * NEAR + 1, 2, 4, 128), f32), vmem((3, 2 * FAR + 1, 3, 4, 128), f32),
            vmem((6, 128), f32), vmem((6, 128), f32),
            vmem((4 * nx, 1, 128), f32), vmem((nz // 4, 1, 128), f32),
            dma((8,)), dma, dma((6,)), dma((6,)), dma((close,)), dma((close,)), dma((wide,)), dma((wide,)), dma, dma,
            dma((4 * nx,)), dma((4 * nx,)), dma((nz // 4,)), dma((nz // 4,)),
        ],
        compiler_params=pltpu.CompilerParams(collective_id=0, has_side_effects=True, vmem_limit_bytes=56 * 2**20),
        name="flow_relax",
    )(sections, tables, skips.T, step_size, mixing, patch_valid, velocity_start)
    return pl.pallas_call(
        unpack_kernel,
        out_shape=(jax.ShapeDtypeStruct((4, 2, 2, 2, 32), f32), jax.ShapeDtypeStruct((4, 2, 2, 32), f32)),
        in_specs=[vm], out_specs=(vm, vm), name="unpack",
    )(packed)


def solution(mesh):
    in_specs = (
        P("gz", "xy", None),
        P("gz", None),
        P("gz", "xy", None),
        P("gz", None, "xy", None),
        P(),
        P(),
    )
    out_specs = (P("gz", None, None, "xy", None), P("gz", None, "xy", None))
    return jax.shard_map(body, mesh=mesh, in_specs=in_specs, out_specs=out_specs, check_vma=False)
```

```python
import functools
import jax
import jax.numpy as jnp
import numpy as np
import ml_dtypes
from jax import lax
from jax.experimental import pallas as pl
from jax.experimental.pallas import tpu as pltpu
from jax.sharding import PartitionSpec as P

PATCH = 64
HALF = 32
ITERS = 3
SHARP = 400.0
STIFF = 0.25
TINY = 1e-06
LOG2E = 1.4426950408889634
SCORE_EXP = SHARP / float(PATCH**4) * LOG2E
MESH = pl.DeviceIdType.MESH
STEPS = 11
NEAR, FAR = 2, 3


def host_tables():
    n = np.arange(PATCH)
    angle = ((n[:, None] * n[None, :]) % PATCH) * (2.0 * np.pi / PATCH)
    rounded = lambda a: np.where(np.abs(a) < 1e-9, 0.0, a).astype(ml_dtypes.bfloat16).astype(np.float64)
    cos, sin = rounded(np.cos(angle)), rounded(np.sin(angle))
    z = np.zeros((PATCH, PATCH))
    forward_cols = np.block([[cos, z, sin, z], [z, cos, z, sin]])
    forward_rows = np.concatenate([cos[:32], cos[32:33], sin[1:32]], axis=0)

    def couple(rr, ri, ir, ii):
        return np.block([[rr, z, ri, z], [z, rr, z, ri], [ir, z, ii, z], [z, ir, z, ii]])

    icols = couple(cos, sin, -sin, cos)
    rr, ri, ir, ii = (np.zeros((PATCH, PATCH)) for _ in range(4))
    rr[0] = cos[0]
    rr[1:32] = 2.0 * cos[1:32]
    ir[1:32] = -2.0 * sin[1:32]
    ir[0] = cos[32]
    ri[32] = cos[32]
    ri[33:] = 2.0 * cos[33:]
    ii[33:] = -2.0 * sin[33:]
    ii[32] = cos[0]
    ipack = couple(rr, ri, ir, ii)
    inverse_rows = np.zeros((64, 64))
    inverse_rows[:, 0] = 1.0
    inverse_rows[:, 1:32] = 2.0 * cos[:, 1:32]
    inverse_rows[:, 32] = cos[:, 32]
    inverse_rows[:, 33:] = -2.0 * sin[:, 1:32]
    last = np.concatenate([forward_rows, z, inverse_rows, z], axis=1)
    return np.concatenate([forward_cols, icols, ipack, last], axis=0).astype(ml_dtypes.bfloat16)


def half_sums(v, left):
    a = jnp.sum(jnp.where(left, v, 0.0), axis=1, keepdims=True)
    b = jnp.sum(jnp.where(left, 0.0, v), axis=1, keepdims=True)
    return jnp.where(left, a, b)


def tile_stats(x_ref, s, a, mean_ref, rs_ref, chunk=512):
    rows = pl.ds(pl.multiple_of(a * PATCH, PATCH), PATCH)
    left = lax.broadcasted_iota(jnp.int32, (1, 128), 1) < 64
    t = s * 2 + a
    scale = 1.0 / PATCH**2
    spans = range(0, chunk, 128)
    for c in range(0, x_ref.shape[2], chunk):
        x = x_ref[s, rows, c:c + chunk].astype(jnp.float32)
        total = jnp.sum(x, axis=0, keepdims=True)
        mean = jnp.concatenate([half_sums(total[:, k:k + 128], left) for k in spans], axis=1) * scale
        mean_ref[t, :, c:c + chunk] = mean
        d = x - mean
        total = jnp.sum(d * d, axis=0, keepdims=True)
        spread = jnp.concatenate([half_sums(total[:, k:k + 128], left) for k in spans], axis=1) * scale
        rs_ref[t, :, c:c + chunk] = lax.rsqrt(spread + 1e-5)


def tile_columns(x_ref, s, a, mean_ref, rs_ref, fcols, half_ref):
    rows = pl.ds(pl.multiple_of(a * PATCH, PATCH), PATCH)
    t = s * 2 + a
    for i in range(x_ref.shape[2] // 128):
        cols = slice(i * 128, (i + 1) * 128)
        x = x_ref[s, rows, cols].astype(jnp.float32)
        normed = ((x - mean_ref[t, :, cols]) * rs_ref[t, :, cols]).astype(jnp.bfloat16)
        half_ref[:, i * 256:(i + 1) * 256] = jnp.dot(normed, fcols, preferred_element_type=jnp.float32).astype(jnp.bfloat16)


def tile_rows(s, a, frows, half_ref, spec_ref):
    lane = lax.broadcasted_iota(jnp.int32, (8, 128), 1) % 64
    row0 = lax.broadcasted_iota(jnp.int32, (8, 128), 0) == 0
    upper = lane >= 32
    for i in range(spec_ref.shape[1]):
        both = jnp.dot(frows, half_ref[:, i * 256:(i + 1) * 256], preferred_element_type=jnp.float32)
        ca, cb = both[:HALF, :128], both[:HALF, 128:]
        sa, sb = both[HALF:, :128], both[HALF:, 128:]
        real, imag = ca - sb, sa + cb
        ca, cb, sa, sb = ca[:8], cb[:8], sa[:8], sb[:8]
        real0 = jnp.where(upper, sa, ca)
        imag0 = jnp.where(upper, sb, cb)
        imag0 = jnp.where(lane == 0, pltpu.roll(ca, 96, axis=1), jnp.where(lane == 32, pltpu.roll(sa, 32, axis=1), imag0))
        real = jnp.concatenate([jnp.where(row0, real0, real[:8]), real[8:]], axis=0)
        imag = jnp.concatenate([jnp.where(row0, imag0, imag[:8]), imag[8:]], axis=0)
        spec_ref[s * 2 + a, i] = jnp.concatenate([real, imag], axis=1).astype(jnp.bfloat16)


def pair_cross(tasks, count, icols, ipack, u_ref):
    lane = lax.broadcasted_iota(jnp.int32, (8, 128), 1) % 32
    row = lax.broadcasted_iota(jnp.int32, (8, 128), 0)
    special = (row == 0) & (lane == 0)
    blocks = []
    for mine_of, other_of in tasks:
        for i in range(count):
            mine, other = mine_of(i).astype(jnp.float32), other_of(i).astype(jnp.float32)
            r, m = mine[:, :128], mine[:, 128:]
            p, q = other[:, :128], other[:, 128:]
            rp, mq = r * p, m * q
            real, imag = rp + mq, m * p - r * q
            real = jnp.concatenate([jnp.where(special, rp[:8], real[:8]), real[8:]], axis=0)
            imag = jnp.concatenate([jnp.where(special, mq[:8], imag[:8]), imag[8:]], axis=0)
            blocks.append(jnp.concatenate([real, imag], axis=1).astype(jnp.bfloat16))
    n = len(blocks)
    inner = jnp.dot(jnp.concatenate(blocks, axis=0), icols, preferred_element_type=jnp.float32)
    first = jnp.dot(jnp.concatenate([b[:16] for b in blocks], axis=0), ipack, preferred_element_type=jnp.float32)
    row0 = lax.broadcasted_iota(jnp.int32, (8, 256), 0) == 0
    for i in range(n):
        head = jnp.where(row0, first[i * 16:i * 16 + 8], inner[i * 32:i * 32 + 8])
        u = jnp.concatenate([head, inner[i * 32 + 8:i * 32 + 32]], axis=0).astype(jnp.bfloat16)
        u_ref[:32, i * 128:(i + 1) * 128] = u[:, :128]
        u_ref[32:, i * 128:(i + 1) * 128] = u[:, 128:]


def pair_soft(u_ref, n, irows, m_ref, z_ref, r_ref, step):
    for h in range(0, n, 2):
        corr = jnp.dot(irows, u_ref[:, h * 128:(h + 2) * 128], preferred_element_type=jnp.float32)
        for i in (h, h + 1):
            e = [corr[8 * r:8 * r + 8, (i - h) * 128:(i - h + 1) * 128] for r in range(8)]
            m = functools.reduce(jnp.maximum, e)
            e = [jnp.exp2((v - m) * SCORE_EXP) for v in e]
            s3 = e[3]
            s2 = e[2] + s3
            s1 = e[1] + s2
            t4 = e[4]
            t5 = t4 + e[5]
            t6 = t5 + e[6]
            t7 = t6 + e[7]
            spot = pl.ds(pl.multiple_of((step * n + i) * 8, 8), 8)
            m_ref[spot] = m
            z_ref[spot] = (s1 + e[0]) + t7
            r_ref[spot] = ((s1 + s2) + s3) - ((t4 + t5) + (t6 + t7))


def pair_finish(m_ref, z_ref, r_ref, first, count):
    rows = count * 32
    lane = lax.broadcasted_iota(jnp.int32, (rows, 128), 1)
    left = lane < 64
    t2 = lane % 64
    shift = jnp.where(t2 < 32, t2, t2 - 64).astype(jnp.float32)
    pick = lambda ref, r: ref[pl.ds(first * 256 + r, rows, stride=8), :]
    top = functools.reduce(jnp.maximum, [pick(m_ref, r) for r in range(8)])
    a = jnp.max(jnp.where(left, top, -jnp.inf), axis=1, keepdims=True)
    b = jnp.max(jnp.where(left, -jnp.inf, top), axis=1, keepdims=True)
    peak = jnp.where(left, a, b)
    beyond = jnp.zeros((rows, 128), jnp.float32)
    stairs = jnp.zeros((rows, 128), jnp.float32)
    eights = jnp.zeros((rows, 128), jnp.float32)
    for r in range(7, -1, -1):
        w = jnp.exp2((pick(m_ref, r) - peak) * SCORE_EXP)
        beyond += w * pick(z_ref, r)
        eights += w * pick(r_ref, r)
        if r > 0:
            stairs += beyond
    total, along = beyond, 8.0 * eights + stairs
    across = total * shift

    def sides(v):
        return (jnp.sum(jnp.where(left, v, 0.0), axis=1, keepdims=True), jnp.sum(jnp.where(left, 0.0, v), axis=1, keepdims=True))

    owner = lax.broadcasted_iota(jnp.int32, (rows, 128), 0) % 32
    mine = (lane % 64) // 2 == owner
    odd = lane % 2 == 1
    (tl, tr), (al, ar), (cl, cr) = sides(total), sides(along), sides(across)
    down = jnp.where(mine, jnp.where(odd, tr, tl), 0.0)
    up = jnp.where(mine, jnp.where(left, jnp.where(odd, ar, al), jnp.where(odd, cr, cl)), 0.0)
    fold = lambda v: [jnp.sum(v[k * 32:(k + 1) * 32], axis=0, keepdims=True) for k in range(count)]
    return [u / d for u, d in zip(fold(up), fold(down))]


def halo(reach):
    return [(db, dx) for dx in (0, -1, 1) for db in range(-reach, reach + 1)
            if (db, dx) != (0, 0) and abs(db) + abs(dx) <= reach]


def shifted(x, by):
    return pltpu.roll(x, (-by) % x.shape[0], axis=0)


def edge_base(k):
    return 5 + 3 * k - k * (k - 1) // 2


def kernel(nz, nx, x_hbm, tab_hbm, skip_hbm, step_hbm, mix_hbm, valid_hbm, start_hbm, out_ref,
           skip_ref, step_ref, mix_ref, valid_ref, start_ref, x_ref, tab_ref, mean_ref, rs_ref, half_ref, spec_ref, recv_ref, u_ref, m_ref, z_ref, r_ref,
           u2_ref, ext_ref, push_ref, back_ref, sent_ref, part1, part2,
           sem_in, sem_x, sem_tab, sem_s, got_s, sem_e, got_e, sem_l, got_l, sem_b, got_b, sem_1, got_1, sem_2, got_2, known):
    gz = lax.axis_index("gz")
    xy = lax.axis_index("xy")
    groups = nz // 4
    yy, zc = gz // groups, gz % groups
    couples = spec_ref.shape[1]

    def tile(i):
        half = i // 2
        return half + i % 2 * (3 - 2 * half), i % 2

    def tile_load(i):
        s, a = tile(i)
        part = pl.ds(a * PATCH, PATCH)
        return pltpu.make_async_copy(x_hbm.at[s, part], x_ref.at[s, part], sem_x.at[i])

    loads = [tile_load(i) for i in range(8)]
    loads[0].start()
    small = [(skip_hbm, skip_ref), (valid_hbm, valid_ref), (start_hbm, start_ref), (step_hbm, step_ref), (mix_hbm, mix_ref)]
    small = [pltpu.make_async_copy(a, b, sem_in.at[n]) for n, (a, b) in enumerate(small)]
    for c in small + loads[1:]:
        c.start()
    tab_load = pltpu.make_async_copy(tab_hbm, tab_ref, sem_tab)
    tab_load.start()

    def at(db, dx):
        return (lax.rem(gz + db + nz, nz), lax.rem(xy + dx + nx, nx))

    def near(r):
        k = lax.rem(yy * nx + xy + r, 4 * nx)
        return (k // nx * groups + zc, lax.rem(k, nx))

    def along(r):
        return (yy * groups + lax.rem(zc + r, groups), xy)

    wide, close = halo(FAR), halo(NEAR)
    barrier = pltpu.get_barrier_semaphore()
    def plane(dx, dy):
        return (lax.rem(yy + dy + 4, 4) * groups + zc, lax.rem(xy + dx + nx, nx))

    corners = [plane(dx, dy) for dx in (-1, 1) for dy in (-1, 1)]
    ends = [along(r) for r in (4, groups - 4)]
    peers = [at(db, dx) for db, dx in wide] + corners + [plane(0, -1), plane(0, 1)]
    peers += [along(r) for k in range(1, 5) for r in (k, groups - k)]
    for peer in peers:
        pl.semaphore_signal(barrier, inc=1, device_id=peer, device_id_type=MESH)

    for c in small:
        c.wait()
    lanes = lax.broadcasted_iota(jnp.int32, (1, 128), 1)
    skip = [[skip_ref[j, s] for j in range(2)] for s in range(4)]
    live = [[(k > 0) & (gz * 4 + s + k < 4 * nz) for k in skip[s]] for s in range(4)]
    for s in range(4):
        ext_ref[1, NEAR, 0, s:s + 1, :] = jnp.concatenate(
            [start_ref[s, c, a:a + 1, :] for c in range(2) for a in range(2)], axis=1)
        row = jnp.concatenate([valid_ref[s, a:a + 1, :] for a in range(2)] * 2, axis=1).astype(jnp.float32)
        for d in (1, 2, 3):
            hit = ((skip[s][0] == d) & live[s][0]) | ((skip[s][1] == d) & live[s][1])
            row = jnp.where(lanes == 63 + d, jnp.where(hit, 1.0, 0.0), row)
        ext_ref[1, NEAR, 1, s:s + 1, :] = row

    def stats(i):
        tile_stats(x_ref, *tile(i), mean_ref, rs_ref)

    def columns(i):
        tile_columns(x_ref, *tile(i), mean_ref, rs_ref, tab_ref[0:128], half_ref)

    def rows(i):
        tile_rows(*tile(i), tab_ref[640:704, 0:64], half_ref, spec_ref)

    def spectrum_copy(i):
        s, a = tile(i)
        slot = s + 2 * a
        return pltpu.make_async_remote_copy(
            src_ref=spec_ref.at[s * 2 + a], dst_ref=recv_ref.at[slot], send_sem=sem_s.at[slot], recv_sem=got_s.at[slot],
            device_id=(lax.rem(gz + nz - 1 + 2 * a, nz), xy), device_id_type=MESH)

    loads[0].wait()
    stats(0)
    loads[1].wait()
    stats(1)
    tab_load.wait()
    columns(0)
    for c in loads[2:]:
        c.wait()
    pl.semaphore_wait(barrier, len(peers))
    for peer in corners + ends:
        pl.semaphore_signal(known, inc=1, device_id=peer, device_id_type=MESH)
    early = []
    for n, (db, dx) in enumerate(close):
        early.append(pltpu.make_async_remote_copy(
            src_ref=ext_ref.at[1, NEAR], dst_ref=ext_ref.at[dx + 1, db + NEAR], send_sem=sem_e.at[n], recv_sem=got_e.at[n],
            device_id=at(-db, -dx), device_id_type=MESH))
        early[-1].start()

    def forward(i, _):
        rows(i - 2)
        columns(i - 1)
        stats(i)
        spectrum_copy(i - 2).start()
        return 0

    lax.fori_loop(2, 8, forward, 0)
    rows(6)
    columns(7)
    rows(7)

    def cross(step, tasks):
        pair_cross(tasks, couples, tab_ref[128:384], tab_ref[384:640], (u_ref, u2_ref)[step % 2])

    def soft(step):
        pair_soft((u_ref, u2_ref)[step % 2], 2 * couples, tab_ref[640:704, 128:192], m_ref, z_ref, r_ref, step)

    def own(s, a):
        return lambda i: spec_ref[s * 2 + a, i]

    def got(slot):
        return lambda i: recv_ref[slot, i]

    def first_section(j):
        p = skip_ref[j, 0]
        cross(j, [(own(0, 0), own(p, 0)), (own(0, 1), own(p, 1))])

    def inside_block(i):
        s, p = i // 2, i - i // 4
        cross(i, [(own(s, 0), own(p, 0)), (own(s, 1), own(p, 1))])

    def over_edge(k, q):
        cross(edge_base(k) + q, [(own(k + 1 + q, 0), got(k)), (got(5 - k), own(q, 1))])

    first_section(0)
    soft(0)
    first_section(1)

    def inside_step(i, _):
        soft(i - 1)
        inside_block(i)
        return 0

    for i in range(2, 5):
        inside_step(i, 0)
    for k in range(2):
        spectrum_copy(2 * k).wait_recv()
        spectrum_copy(2 * k + 1).wait_recv()

        def edge_step(q, _, k=k):
            soft(edge_base(k) + q - 1)
            over_edge(k, q)
            return 0

        for q in range(3 - k):
            edge_step(q, 0)

    for c in early:
        c.wait_recv()
    blocks = 2 * NEAR + 1
    size = 4 * blocks + 4
    here = slice(4 * NEAR, 4 * NEAR + 4)
    lane = lax.broadcasted_iota(jnp.int32, (size, 128), 1)
    col = lane % 32
    upper = (lane // 32) % 2 == 0
    inside = [jnp.where(xy > 0, 1.0, 0.0), 1.0, jnp.where(xy < nx - 1, 1.0, 0.0)]
    pad = jnp.zeros((4, 128), jnp.float32)

    def reaches(dx, k):
        return abs(k - NEAR) + abs(dx - 1) <= NEAR

    def gather(dx, f):
        return jnp.concatenate([ext_ref[dx, k, f] if reaches(dx, k) else pad for k in range(blocks)] + [pad], axis=0)

    def springs(dx):
        info = gather(dx, 1)
        valid = jnp.where(lane < 64, info, pltpu.roll(info, 64, axis=1))
        return [info[:, 63 + d:64 + d] * valid * shifted(valid, d) for d in (1, 2, 3)]

    weights = [None, springs(1), None]
    soft(STEPS - 2)
    flows = pair_finish(m_ref, z_ref, r_ref, 0, STEPS - 1)

    low = (lanes // 32) % 2 == 0
    base = 4 * NEAR
    add = [[jnp.zeros((1, 128), jnp.float32) for _ in range(4)] for _ in range(3)]

    def spring(s, d):
        return weights[1][d - 1][base + s:base + s + 1]

    def push(source, target, value):
        for where, sign in ((source, -1.0), (target, 1.0)):
            add[1 + where // 4][where % 4] += sign * value

    for j in range(2):
        for d in (1, 2, 3):
            push(0, d, jnp.where(skip[0][j] == d, spring(0, d), 0.0) * flows[j])
    for i in (2, 3, 4):
        s, p = i // 2, i - i // 4
        push(s, p, spring(s, p - s) * flows[i])
    def push_edge(k, q):
        f = flows[edge_base(k) + q]
        push(k + 1 + q, 4 + k, jnp.where(low, spring(k + 1 + q, 3 - q) * f, 0.0))
        push(-1 - k, q, jnp.where(low, 0.0, spring(-1 - k, 1 + k + q) * f))

    for k in range(2):
        for q in range(3 - k):
            push_edge(k, q)

    spectrum_copy(4).wait_recv()
    spectrum_copy(5).wait_recv()
    over_edge(2, 0)
    soft(STEPS - 1)
    flows += pair_finish(m_ref, z_ref, r_ref, STEPS - 1, 1)
    push_edge(2, 0)

    for k in range(3):
        push_ref[1, FAR, k] = jnp.concatenate(add[k], axis=0)
    late = []
    for n, (db, dx) in enumerate(wide):
        reach = abs(db) + abs(dx)
        low_part = 0 if db > 0 or reach < 2 else (1 if reach < 3 else 2)
        high_part = 3 if db < 0 or reach < 2 else (2 if reach < 3 else 1)
        part = pl.ds(low_part, high_part - low_part)
        late.append(pltpu.make_async_remote_copy(
            src_ref=push_ref.at[1, FAR, part], dst_ref=push_ref.at[dx + 1, db + FAR, part],
            send_sem=sem_l.at[n], recv_sem=got_l.at[n], device_id=at(-db, -dx), device_id_type=MESH))
        late[-1].start()

    for k in range(6):
        sent_ref[k:k + 1, :] = flows[5 + k]
    back = pltpu.make_async_remote_copy(
        src_ref=sent_ref, dst_ref=back_ref, send_sem=sem_b, recv_sem=got_b, device_id=at(-1, 0), device_id_type=MESH)
    back.start()

    weights = [springs(0), weights[1], springs(2)]
    vel = [gather(dx, 0) * inside[dx] for dx in range(3)]

    def force(fields, dx):
        v = fields[dx]
        above = fields[dx - 1] if dx > 0 else jnp.zeros_like(v)
        below = fields[dx + 1] if dx < 2 else jnp.zeros_like(v)
        lateral = jnp.where(col == 0, 0.0, pltpu.roll(v, 1, axis=1)) + jnp.where(col == 31, 0.0, pltpu.roll(v, 127, axis=1))
        down, up = pltpu.roll(v, 32, axis=1), pltpu.roll(v, 96, axis=1)
        vertical = jnp.where(upper, pltpu.roll(above, 96, axis=1) + up, down + pltpu.roll(below, 32, axis=1))
        out = STIFF * (lateral + vertical - 4.0 * v)
        for d in (1, 2, 3):
            pull = weights[dx][d - 1] * (shifted(v, d) - v)
            out += pull - shifted(pull, -d)
        return out * inside[dx]

    av = [force(vel, dx) for dx in range(3)]
    aav = force(av, 1)
    for c in late:
        c.wait_recv()
    bias = []
    for dx in range(3):
        parts = [push_ref[dx, k + 1, 1] + push_ref[dx, k, 2] + push_ref[dx, k + 2, 0] if reaches(dx, k) else pad
                 for k in range(blocks)]
        bias.append(jnp.concatenate(parts + [pad], axis=0) * inside[dx])
    ab = [force(bias, dx) for dx in range(3)]
    aab = force(ab, 1)
    basis = [x[here] for x in (vel[1], bias[1], av[1], ab[1], aav, aab)]

    index, sums = {}, []
    for i in range(6):
        for j in range(i, 6):
            index[i, j] = index[j, i] = len(sums)
            sums.append(jnp.sum(basis[i] * basis[j], axis=0, keepdims=True))
    sums = jnp.sum(jnp.concatenate(sums + [jnp.zeros((3, 128), jnp.float32)], axis=0), axis=1, keepdims=True)
    diagonal = lax.broadcasted_iota(jnp.int32, (24, 128), 0) == lax.broadcasted_iota(jnp.int32, (24, 128), 1)
    part1[0] = jnp.sum(jnp.where(diagonal, sums, 0.0), axis=0, keepdims=True)

    def scatter(part, count, peer, sem, got):
        sends = []
        for r in range(1, count):
            sends.append(pltpu.make_async_remote_copy(
                src_ref=part.at[0], dst_ref=part.at[r], send_sem=sem.at[r], recv_sem=got.at[r],
                device_id=peer(r), device_id_type=MESH))
            sends[-1].start()
        return sends

    def collect(part, sends):
        for c in sends:
            c.wait_recv()
        return functools.reduce(jnp.add, [part[r] for r in range(len(sends) + 1)])

    pl.semaphore_wait(known, len(corners + ends))
    sends1 = scatter(part1, 4 * nx, near, sem_1, got_1)

    back.wait_recv()

    def flow_at(s, d):
        if s + d < 4:
            return flows[2 * s - 1 + d if s == 1 else 4]
        far = flows[edge_base(s + d - 4) + 3 - d]
        row = edge_base(3 - s) + s + d - 4 - 5
        return jnp.where(low, far, back_ref[row:row + 1, :])

    for s in range(4):
        for j in range(2):
            if s == 0:
                f = flows[j]
            else:
                f = flow_at(s, 3)
                for d in (1, 2):
                    f = jnp.where(skip[s][j] == d, flow_at(s, d), f)
            out_ref[2 * s + j:2 * s + j + 1, :] = jnp.where(live[s][j], f, 0.0)

    for i in range(6):
        spectrum_copy(i).wait_send()
    for c in early + late + [back]:
        c.wait_send()
    part2[0] = collect(part1, sends1)
    sends2 = scatter(part2, groups, along, sem_2, got_2)
    gram = collect(part2, sends2)
    g = {k: jnp.broadcast_to(gram[:, n:n + 1], (1, 128)) for k, n in index.items()}

    def dot(p, q):
        terms = [p[i] * q[j] * g[i, j] for i in range(6) for j in range(6) if p[i] is not None and q[j] is not None]
        return functools.reduce(jnp.add, terms)

    def plus(*xs):
        xs = [x for x in xs if x is not None]
        return functools.reduce(jnp.add, xs) if xs else None

    def times(k, x):
        return None if x is None else k * x

    one = jnp.ones((1, 128), jnp.float32)
    v = [one] + [None] * 5
    d = [None] * 6
    for it in range(ITERS):
        f = [None, one] + d[:4]
        power, speed, strength = dot(f, v), dot(v, v), dot(f, f)
        speed, strength = jnp.maximum(speed, 0.0), jnp.maximum(strength, 0.0)
        gating = 0.5 + 0.5 * power / jnp.sqrt((speed + TINY) * (strength + TINY))
        ratio = jnp.sqrt((speed + TINY) / (strength + TINY))
        mix, step = mix_ref[it], step_ref[it]
        kv, kf = gating * (1.0 - mix), gating * (mix * ratio) + step
        v = [plus(times(kv, v[i]), times(kf, f[i])) for i in range(6)]
        d = [plus(d[i], times(step, v[i])) for i in range(6)]
    result = functools.reduce(jnp.add, [d[i] * basis[i] for i in range(6)])
    out_ref[8:12, :] = result

    for c in sends1 + sends2:
        c.wait_send()


def unpack_kernel(packed_ref, flow_ref, displace_ref):
    for c in range(2):
        for a in range(2):
            lanes = slice(c * 64 + a * 32, c * 64 + a * 32 + 32)
            for s in range(4):
                displace_ref[s, c, a:a + 1, :] = packed_ref[8 + s:9 + s, lanes]
                for j in range(2):
                    flow_ref[s, j, c, a:a + 1, :] = packed_ref[2 * s + j:2 * s + j + 1, lanes]


def body(sections, skips, patch_valid, velocity_start, step_size, mixing):
    nz, nx = lax.axis_size("gz"), lax.axis_size("xy")
    vm, hbm = (pl.BlockSpec(memory_space=k) for k in (pltpu.VMEM, pl.ANY))
    tables = jnp.asarray(host_tables())
    width = sections.shape[2]
    couples = width // 128
    dma = pltpu.SemaphoreType.DMA
    wide, close = len(halo(FAR)), len(halo(NEAR))
    f32, bf16 = jnp.float32, jnp.bfloat16
    vmem = pltpu.VMEM
    packed = pl.pallas_call(
        functools.partial(kernel, nz, nx),
        out_shape=jax.ShapeDtypeStruct((12, 128), f32),
        in_specs=[hbm] * 7, out_specs=vm,
        scratch_shapes=[
            pltpu.SMEM((2, 4), jnp.int32), pltpu.SMEM((3,), f32), pltpu.SMEM((3,), f32),
            vmem(patch_valid.shape, jnp.int32), vmem(velocity_start.shape, f32),
            vmem(sections.shape, bf16), vmem(tables.shape, bf16),
            vmem((8, 1, width), f32), vmem((8, 1, width), f32),
            vmem((64, couples * 256), bf16),
            vmem((8, couples, HALF, 256), bf16), vmem((6, couples, HALF, 256), bf16),
            vmem((64, couples * 256), bf16),
            vmem((STEPS * couples * 16, 128), f32), vmem((STEPS * couples * 16, 128), f32), vmem((STEPS * couples * 16, 128), f32),
            vmem((64, couples * 256), bf16),
            vmem((3, 2 * NEAR + 1, 2, 4, 128), f32), vmem((3, 2 * FAR + 1, 3, 4, 128), f32),
            vmem((6, 128), f32), vmem((6, 128), f32),
            vmem((4 * nx, 1, 128), f32), vmem((nz // 4, 1, 128), f32),
            dma((5,)), dma((8,)), dma, dma((6,)), dma((6,)), dma((close,)), dma((close,)), dma((wide,)), dma((wide,)), dma, dma,
            dma((4 * nx,)), dma((4 * nx,)), dma((nz // 4,)), dma((nz // 4,)),
            pltpu.SemaphoreType.REGULAR,
        ],
        compiler_params=pltpu.CompilerParams(collective_id=0, has_side_effects=True, vmem_limit_bytes=56 * 2**20),
        name="flow_relax",
    )(sections, tables, skips.T, step_size, mixing, patch_valid, velocity_start)
    return pl.pallas_call(
        unpack_kernel,
        out_shape=(jax.ShapeDtypeStruct((4, 2, 2, 2, 32), f32), jax.ShapeDtypeStruct((4, 2, 2, 32), f32)),
        in_specs=[vm], out_specs=(vm, vm), name="unpack",
    )(packed)


def solution(mesh):
    in_specs = (
        P("gz", "xy", None),
        P("gz", None),
        P("gz", "xy", None),
        P("gz", None, "xy", None),
        P(),
        P(),
    )
    out_specs = (P("gz", None, None, "xy", None), P("gz", None, "xy", None))
    return jax.shard_map(body, mesh=mesh, in_specs=in_specs, out_specs=out_specs, check_vma=False)
```

```python
import functools
import jax
import jax.numpy as jnp
import numpy as np
import ml_dtypes
from jax import lax
from jax.experimental import pallas as pl
from jax.experimental.pallas import tpu as pltpu
from jax.sharding import PartitionSpec as P

PATCH = 64
HALF = 32
ITERS = 3
SHARP = 400.0
STIFF = 0.25
TINY = 1e-06
LOG2E = 1.4426950408889634
SCORE_EXP = SHARP / float(PATCH**4) * LOG2E
MESH = pl.DeviceIdType.MESH
EARLY = 5
STEPS = [
    [(0, 0, "s0"), (1, 0, "s0")],
    [(0, 0, "s1"), (1, 0, "s1")],
    [(1, 1, 1), (1, 1, 2)],
    [(0, 1, "s0"), (1, 2, 1)],
    [(0, 1, "s1"), (2, 3, 1)],
    [(0, 3, 1), (2, 3, 2)],
    [(0, 2, "s0"), (2, 3, 3)],
    [(0, 2, "s1"), (2, 2, 2)],
    [(0, 3, 2), (2, 2, 3)],
    [(0, 3, 3), (2, 1, 3)],
]
ARRIVALS = [3, 6, 9]
SEND = 2
SPRINGS_BACK = [(3, 1), (3, 2), (3, 3), (2, 2), (2, 3), (1, 3)]
NEAR, FAR = 2, 3


def host_tables():
    n = np.arange(PATCH)
    angle = ((n[:, None] * n[None, :]) % PATCH) * (2.0 * np.pi / PATCH)
    rounded = lambda a: np.where(np.abs(a) < 1e-9, 0.0, a).astype(ml_dtypes.bfloat16).astype(np.float64)
    cos, sin = rounded(np.cos(angle)), rounded(np.sin(angle))
    z = np.zeros((PATCH, PATCH))
    forward_cols = np.block([[cos, z, sin, z], [z, cos, z, sin]])
    forward_rows = np.concatenate([cos[:32], cos[32:33], sin[1:32]], axis=0)

    def couple(rr, ri, ir, ii):
        return np.block([[rr, z, ri, z], [z, rr, z, ri], [ir, z, ii, z], [z, ir, z, ii]])

    icols = couple(cos, sin, -sin, cos)
    rr, ri, ir, ii = (np.zeros((PATCH, PATCH)) for _ in range(4))
    rr[0] = cos[0]
    rr[1:32] = 2.0 * cos[1:32]
    ir[1:32] = -2.0 * sin[1:32]
    ir[0] = cos[32]
    ri[32] = cos[32]
    ri[33:] = 2.0 * cos[33:]
    ii[33:] = -2.0 * sin[33:]
    ii[32] = cos[0]
    ipack = couple(rr, ri, ir, ii)
    inverse_rows = np.zeros((64, 64))
    inverse_rows[:, 0] = 1.0
    inverse_rows[:, 1:32] = 2.0 * cos[:, 1:32]
    inverse_rows[:, 32] = cos[:, 32]
    inverse_rows[:, 33:] = -2.0 * sin[:, 1:32]
    last = np.concatenate([forward_rows, z, inverse_rows, z], axis=1)
    return np.concatenate([forward_cols, icols, ipack, last], axis=0).astype(ml_dtypes.bfloat16)


def half_sums(v, left):
    a = jnp.sum(jnp.where(left, v, 0.0), axis=1, keepdims=True)
    b = jnp.sum(jnp.where(left, 0.0, v), axis=1, keepdims=True)
    return jnp.where(left, a, b)


def tile_stats(x_ref, s, a, mean_ref, rs_ref, chunk=512):
    rows = pl.ds(pl.multiple_of(a * PATCH, PATCH), PATCH)
    left = lax.broadcasted_iota(jnp.int32, (1, 128), 1) < 64
    t = s * 2 + a
    scale = 1.0 / PATCH**2
    spans = range(0, chunk, 128)
    for c in range(0, x_ref.shape[2], chunk):
        x = x_ref[s, rows, c:c + chunk].astype(jnp.float32)
        total = jnp.sum(x, axis=0, keepdims=True)
        mean = jnp.concatenate([half_sums(total[:, k:k + 128], left) for k in spans], axis=1) * scale
        mean_ref[t, :, c:c + chunk] = mean
        d = x - mean
        total = jnp.sum(d * d, axis=0, keepdims=True)
        spread = jnp.concatenate([half_sums(total[:, k:k + 128], left) for k in spans], axis=1) * scale
        rs_ref[t, :, c:c + chunk] = lax.rsqrt(spread + 1e-5)


def tile_columns(x_ref, s, a, mean_ref, rs_ref, fcols, half_ref):
    rows = pl.ds(pl.multiple_of(a * PATCH, PATCH), PATCH)
    t = s * 2 + a
    for i in range(x_ref.shape[2] // 128):
        cols = slice(i * 128, (i + 1) * 128)
        x = x_ref[s, rows, cols].astype(jnp.float32)
        normed = ((x - mean_ref[t, :, cols]) * rs_ref[t, :, cols]).astype(jnp.bfloat16)
        half_ref[:, i * 256:(i + 1) * 256] = jnp.dot(normed, fcols, preferred_element_type=jnp.float32).astype(jnp.bfloat16)


def tile_rows(s, a, frows, half_ref, spec_ref):
    lane = lax.broadcasted_iota(jnp.int32, (8, 128), 1) % 64
    row0 = lax.broadcasted_iota(jnp.int32, (8, 128), 0) == 0
    upper = lane >= 32
    for i in range(spec_ref.shape[1]):
        both = jnp.dot(frows, half_ref[:, i * 256:(i + 1) * 256], preferred_element_type=jnp.float32)
        ca, cb = both[:HALF, :128], both[:HALF, 128:]
        sa, sb = both[HALF:, :128], both[HALF:, 128:]
        real, imag = ca - sb, sa + cb
        ca, cb, sa, sb = ca[:8], cb[:8], sa[:8], sb[:8]
        real0 = jnp.where(upper, sa, ca)
        imag0 = jnp.where(upper, sb, cb)
        imag0 = jnp.where(lane == 0, pltpu.roll(ca, 96, axis=1), jnp.where(lane == 32, pltpu.roll(sa, 32, axis=1), imag0))
        real = jnp.concatenate([jnp.where(row0, real0, real[:8]), real[8:]], axis=0)
        imag = jnp.concatenate([jnp.where(row0, imag0, imag[:8]), imag[8:]], axis=0)
        spec_ref[s * 2 + a, i] = jnp.concatenate([real, imag], axis=1).astype(jnp.bfloat16)


def pair_cross(tasks, count, icols, ipack, u_ref):
    lane = lax.broadcasted_iota(jnp.int32, (8, 128), 1) % 32
    row = lax.broadcasted_iota(jnp.int32, (8, 128), 0)
    special = (row == 0) & (lane == 0)
    blocks = []
    for mine_of, other_of in tasks:
        for i in range(count):
            mine, other = mine_of(i).astype(jnp.float32), other_of(i).astype(jnp.float32)
            r, m = mine[:, :128], mine[:, 128:]
            p, q = other[:, :128], other[:, 128:]
            rp, mq = r * p, m * q
            real, imag = rp + mq, m * p - r * q
            real = jnp.concatenate([jnp.where(special, rp[:8], real[:8]), real[8:]], axis=0)
            imag = jnp.concatenate([jnp.where(special, mq[:8], imag[:8]), imag[8:]], axis=0)
            blocks.append(jnp.concatenate([real, imag], axis=1).astype(jnp.bfloat16))
    n = len(blocks)
    inner = jnp.dot(jnp.concatenate(blocks, axis=0), icols, preferred_element_type=jnp.float32)
    first = jnp.dot(jnp.concatenate([b[:16] for b in blocks], axis=0), ipack, preferred_element_type=jnp.float32)
    row0 = lax.broadcasted_iota(jnp.int32, (8, 256), 0) == 0
    for i in range(n):
        head = jnp.where(row0, first[i * 16:i * 16 + 8], inner[i * 32:i * 32 + 8])
        u = jnp.concatenate([head, inner[i * 32 + 8:i * 32 + 32]], axis=0).astype(jnp.bfloat16)
        u_ref[:32, i * 128:(i + 1) * 128] = u[:, :128]
        u_ref[32:, i * 128:(i + 1) * 128] = u[:, 128:]


def pair_soft(u_ref, n, irows, m_ref, z_ref, r_ref, step):
    for h in range(0, n, 2):
        corr = jnp.dot(irows, u_ref[:, h * 128:(h + 2) * 128], preferred_element_type=jnp.float32)
        for i in (h, h + 1):
            e = [corr[8 * r:8 * r + 8, (i - h) * 128:(i - h + 1) * 128] for r in range(8)]
            m = functools.reduce(jnp.maximum, e)
            e = [jnp.exp2((v - m) * SCORE_EXP) for v in e]
            s3 = e[3]
            s2 = e[2] + s3
            s1 = e[1] + s2
            t4 = e[4]
            t5 = t4 + e[5]
            t6 = t5 + e[6]
            t7 = t6 + e[7]
            spot = pl.ds(pl.multiple_of((step * n + i) * 8, 8), 8)
            m_ref[spot] = m
            z_ref[spot] = (s1 + e[0]) + t7
            r_ref[spot] = ((s1 + s2) + s3) - ((t4 + t5) + (t6 + t7))


def pair_finish(m_ref, z_ref, r_ref, first, count):
    rows = count * 32
    lane = lax.broadcasted_iota(jnp.int32, (rows, 128), 1)
    left = lane < 64
    t2 = lane % 64
    shift = jnp.where(t2 < 32, t2, t2 - 64).astype(jnp.float32)
    pick = lambda ref, r: ref[pl.ds(first * 256 + r, rows, stride=8), :]
    top = functools.reduce(jnp.maximum, [pick(m_ref, r) for r in range(8)])
    a = jnp.max(jnp.where(left, top, -jnp.inf), axis=1, keepdims=True)
    b = jnp.max(jnp.where(left, -jnp.inf, top), axis=1, keepdims=True)
    peak = jnp.where(left, a, b)
    beyond = jnp.zeros((rows, 128), jnp.float32)
    stairs = jnp.zeros((rows, 128), jnp.float32)
    eights = jnp.zeros((rows, 128), jnp.float32)
    for r in range(7, -1, -1):
        w = jnp.exp2((pick(m_ref, r) - peak) * SCORE_EXP)
        beyond += w * pick(z_ref, r)
        eights += w * pick(r_ref, r)
        if r > 0:
            stairs += beyond
    total, along = beyond, 8.0 * eights + stairs
    across = total * shift

    def sides(v):
        return (jnp.sum(jnp.where(left, v, 0.0), axis=1, keepdims=True), jnp.sum(jnp.where(left, 0.0, v), axis=1, keepdims=True))

    owner = lax.broadcasted_iota(jnp.int32, (rows, 128), 0) % 32
    mine = (lane % 64) // 2 == owner
    odd = lane % 2 == 1
    (tl, tr), (al, ar), (cl, cr) = sides(total), sides(along), sides(across)
    down = jnp.where(mine, jnp.where(odd, tr, tl), 0.0)
    up = jnp.where(mine, jnp.where(left, jnp.where(odd, ar, al), jnp.where(odd, cr, cl)), 0.0)
    fold = lambda v: [jnp.sum(v[k * 32:(k + 1) * 32], axis=0, keepdims=True) for k in range(count)]
    return [u / d for u, d in zip(fold(up), fold(down))]


def halo(reach):
    return [(db, dx) for dx in (0, -1, 1) for db in range(-reach, reach + 1)
            if (db, dx) != (0, 0) and abs(db) + abs(dx) <= reach]


def shifted(x, by):
    return pltpu.roll(x, (-by) % x.shape[0], axis=0)


def kernel(nz, nx, x_hbm, tab_hbm, skip_hbm, step_hbm, mix_hbm, valid_hbm, start_hbm, out_ref,
           skip_ref, step_ref, mix_ref, valid_ref, start_ref, x_ref, tab_ref, mean_ref, rs_ref, half_ref, spec_ref, recv_ref, u_ref, m_ref, z_ref, r_ref,
           u2_ref, ext_ref, push_ref, back_ref, sent_ref, part1, part2,
           sem_in, sem_x, sem_tab, sem_s, got_s, sem_e, got_e, sem_l, got_l, sem_b, got_b, sem_1, got_1, sem_2, got_2, known):
    gz = lax.axis_index("gz")
    xy = lax.axis_index("xy")
    groups = nz // 4
    yy, zc = gz // groups, gz % groups
    couples = spec_ref.shape[1]

    def tile(i):
        half = i // 2
        return half + i % 2 * (3 - 2 * half), i % 2

    def tile_load(i):
        s, a = tile(i)
        part = pl.ds(a * PATCH, PATCH)
        return pltpu.make_async_copy(x_hbm.at[s, part], x_ref.at[s, part], sem_x.at[i])

    loads = [tile_load(i) for i in range(8)]
    loads[0].start()
    small = [(skip_hbm, skip_ref), (valid_hbm, valid_ref), (start_hbm, start_ref), (step_hbm, step_ref), (mix_hbm, mix_ref)]
    small = [pltpu.make_async_copy(a, b, sem_in.at[n]) for n, (a, b) in enumerate(small)]
    for c in small + loads[1:]:
        c.start()
    tab_load = pltpu.make_async_copy(tab_hbm, tab_ref, sem_tab)
    tab_load.start()

    def at(db, dx):
        return (lax.rem(gz + db + nz, nz), lax.rem(xy + dx + nx, nx))

    def near(r):
        k = lax.rem(yy * nx + xy + r, 4 * nx)
        return (k // nx * groups + zc, lax.rem(k, nx))

    def along(r):
        return (yy * groups + lax.rem(zc + r, groups), xy)

    wide, close = halo(FAR), halo(NEAR)
    barrier = pltpu.get_barrier_semaphore()
    def plane(dx, dy):
        return (lax.rem(yy + dy + 4, 4) * groups + zc, lax.rem(xy + dx + nx, nx))

    corners = [plane(dx, dy) for dx in (-1, 1) for dy in (-1, 1)]
    ends = [along(r) for r in (4, groups - 4)]
    peers = [at(db, dx) for db, dx in wide] + corners + [plane(0, -1), plane(0, 1)]
    peers += [along(r) for k in range(1, 5) for r in (k, groups - k)]
    for peer in peers:
        pl.semaphore_signal(barrier, inc=1, device_id=peer, device_id_type=MESH)

    for c in small:
        c.wait()
    lanes = lax.broadcasted_iota(jnp.int32, (1, 128), 1)
    skip = [[skip_ref[j, s] for j in range(2)] for s in range(4)]
    live = [[(k > 0) & (gz * 4 + s + k < 4 * nz) for k in skip[s]] for s in range(4)]
    for s in range(4):
        ext_ref[1, NEAR, 0, s:s + 1, :] = jnp.concatenate(
            [start_ref[s, c, a:a + 1, :] for c in range(2) for a in range(2)], axis=1)
        row = jnp.concatenate([valid_ref[s, a:a + 1, :] for a in range(2)] * 2, axis=1).astype(jnp.float32)
        for d in (1, 2, 3):
            hit = ((skip[s][0] == d) & live[s][0]) | ((skip[s][1] == d) & live[s][1])
            row = jnp.where(lanes == 63 + d, jnp.where(hit, 1.0, 0.0), row)
        ext_ref[1, NEAR, 1, s:s + 1, :] = row

    def stats(i):
        tile_stats(x_ref, *tile(i), mean_ref, rs_ref)

    def columns(i):
        tile_columns(x_ref, *tile(i), mean_ref, rs_ref, tab_ref[0:128], half_ref)

    def rows(i):
        tile_rows(*tile(i), tab_ref[640:704, 0:64], half_ref, spec_ref)

    def spectrum_copy(i):
        s, a = tile(i)
        slot = s + 2 * a
        return pltpu.make_async_remote_copy(
            src_ref=spec_ref.at[s * 2 + a], dst_ref=recv_ref.at[slot], send_sem=sem_s.at[slot], recv_sem=got_s.at[slot],
            device_id=(lax.rem(gz + nz - 1 + 2 * a, nz), xy), device_id_type=MESH)

    loads[0].wait()
    stats(0)
    tab_load.wait()
    columns(0)
    rows(0)
    pl.semaphore_wait(barrier, len(peers))
    spectrum_copy(0).start()
    loads[1].wait()
    stats(1)
    columns(1)
    rows(1)
    spectrum_copy(1).start()
    for peer in corners + ends:
        pl.semaphore_signal(known, inc=1, device_id=peer, device_id_type=MESH)
    early = []
    for n, (db, dx) in enumerate(close):
        early.append(pltpu.make_async_remote_copy(
            src_ref=ext_ref.at[1, NEAR], dst_ref=ext_ref.at[dx + 1, db + NEAR], send_sem=sem_e.at[n], recv_sem=got_e.at[n],
            device_id=at(-db, -dx), device_id_type=MESH))
        early[-1].start()
    for c in loads[2:]:
        c.wait()
    stats(2)
    stats(3)
    columns(2)

    def forward(i, _):
        rows(i - 2)
        columns(i - 1)
        stats(i)
        return 0

    lax.fori_loop(4, 8, forward, 0)
    spectrum_copy(2).start()
    spectrum_copy(3).start()
    rows(6)
    columns(7)
    rows(7)

    def own(s, a):
        return lambda i: spec_ref[s * 2 + a, i]

    def got(slot):
        return lambda i: recv_ref[slot, i]

    def task(kind, s, what):
        if kind == 2:
            return got(2 + s), own(s + what - 4, 1)
        if what not in ("s0", "s1"):
            return own(s, kind), got(s + what - 4) if s + what > 3 else own(s + what, kind)
        d = skip_ref[int(what[1]), s]
        if s == 0:
            return own(0, kind), own(d, kind)
        if s == 1:
            inner = own(jnp.minimum(d + 1, 3), kind)
            return own(1, kind), lambda i: jnp.where(d == 3, recv_ref[0, i], inner(i))
        return own(2, kind), lambda i: jnp.where(d == 1, spec_ref[6 + kind, i], jnp.where(d == 2, recv_ref[0, i], recv_ref[1, i]))

    def cross(step):
        pair_cross([task(*t) for t in STEPS[step]], couples, tab_ref[128:384], tab_ref[384:640], (u_ref, u2_ref)[step % 2])

    def soft(step):
        pair_soft((u_ref, u2_ref)[step % 2], 2 * couples, tab_ref[640:704, 128:192], m_ref, z_ref, r_ref, step)

    last = len(STEPS) - 1
    flows = []
    cross(0)
    for step in range(1, last):
        if step in ARRIVALS:
            k = ARRIVALS.index(step)
            spectrum_copy(2 * k).wait_recv()
            spectrum_copy(2 * k + 1).wait_recv()
        if step == SEND:
            spectrum_copy(4).start()
            spectrum_copy(5).start()
        soft(step - 1)
        cross(step)
        if step == EARLY:
            flows += pair_finish(m_ref, z_ref, r_ref, 0, EARLY)

    for c in early:
        c.wait_recv()
    blocks = 2 * NEAR + 1
    size = 4 * blocks + 4
    here = slice(4 * NEAR, 4 * NEAR + 4)
    lane = lax.broadcasted_iota(jnp.int32, (size, 128), 1)
    col = lane % 32
    upper = (lane // 32) % 2 == 0
    inside = [jnp.where(xy > 0, 1.0, 0.0), 1.0, jnp.where(xy < nx - 1, 1.0, 0.0)]
    pad = jnp.zeros((4, 128), jnp.float32)

    def reaches(dx, k):
        return abs(k - NEAR) + abs(dx - 1) <= NEAR

    def gather(dx, f):
        return jnp.concatenate([ext_ref[dx, k, f] if reaches(dx, k) else pad for k in range(blocks)] + [pad], axis=0)

    def springs(dx):
        info = gather(dx, 1)
        valid = jnp.where(lane < 64, info, pltpu.roll(info, 64, axis=1))
        return [info[:, 63 + d:64 + d] * valid * shifted(valid, d) for d in (1, 2, 3)]

    weights = [None, springs(1), None]
    soft(last - 1)
    flows += pair_finish(m_ref, z_ref, r_ref, EARLY, last - EARLY)

    low = (lanes // 32) % 2 == 0
    base = 4 * NEAR
    add = [[jnp.zeros((1, 128), jnp.float32) for _ in range(4)] for _ in range(3)]

    def spring(s, d):
        return weights[1][d - 1][base + s:base + s + 1]

    def push(source, target, value):
        for where, sign in ((source, -1.0), (target, 1.0)):
            add[1 + where // 4][where % 4] += sign * value

    def push_step(step):
        for slot, (kind, s, what) in enumerate(STEPS[step]):
            f = flows[step]
            if slot != min(kind, 1):
                f = pltpu.roll(f, 32, axis=1)
            f = jnp.where(low, f, 0.0) if kind == 0 else jnp.where(low, 0.0, f)
            where = s - 4 if kind == 2 else s
            if what in ("s0", "s1"):
                for d in (1, 2, 3):
                    push(where, where + d, jnp.where(skip[s][int(what[1])] == d, spring(where, d), 0.0) * f)
            else:
                push(where, where + what, spring(where, what) * f)

    for step in range(last):
        push_step(step)

    spectrum_copy(4).wait_recv()
    spectrum_copy(5).wait_recv()
    cross(last)
    soft(last)
    flows += pair_finish(m_ref, z_ref, r_ref, last, 1)
    push_step(last)

    for k in range(3):
        push_ref[1, FAR, k] = jnp.concatenate(add[k], axis=0)
    late = []
    for n, (db, dx) in enumerate(wide):
        reach = abs(db) + abs(dx)
        low_part = 0 if db > 0 or reach < 2 else (1 if reach < 3 else 2)
        high_part = 3 if db < 0 or reach < 2 else (2 if reach < 3 else 1)
        part = pl.ds(low_part, high_part - low_part)
        late.append(pltpu.make_async_remote_copy(
            src_ref=push_ref.at[1, FAR, part], dst_ref=push_ref.at[dx + 1, db + FAR, part],
            send_sem=sem_l.at[n], recv_sem=got_l.at[n], device_id=at(-db, -dx), device_id_type=MESH))
        late[-1].start()

    step_of = {t: step for step, tasks in enumerate(STEPS) for t in tasks}
    for n, (s, d) in enumerate(SPRINGS_BACK):
        sent_ref[n:n + 1, :] = flows[step_of[2, s, d]]
    back = pltpu.make_async_remote_copy(
        src_ref=sent_ref, dst_ref=back_ref, send_sem=sem_b, recv_sem=got_b, device_id=at(-1, 0), device_id_type=MESH)
    back.start()

    weights = [springs(0), weights[1], springs(2)]
    vel = [gather(dx, 0) * inside[dx] for dx in range(3)]

    def force(fields, dx):
        v = fields[dx]
        above = fields[dx - 1] if dx > 0 else jnp.zeros_like(v)
        below = fields[dx + 1] if dx < 2 else jnp.zeros_like(v)
        lateral = jnp.where(col == 0, 0.0, pltpu.roll(v, 1, axis=1)) + jnp.where(col == 31, 0.0, pltpu.roll(v, 127, axis=1))
        down, up = pltpu.roll(v, 32, axis=1), pltpu.roll(v, 96, axis=1)
        vertical = jnp.where(upper, pltpu.roll(above, 96, axis=1) + up, down + pltpu.roll(below, 32, axis=1))
        out = STIFF * (lateral + vertical - 4.0 * v)
        for d in (1, 2, 3):
            pull = weights[dx][d - 1] * (shifted(v, d) - v)
            out += pull - shifted(pull, -d)
        return out * inside[dx]

    av = [force(vel, dx) for dx in range(3)]
    aav = force(av, 1)
    for c in late:
        c.wait_recv()
    bias = []
    for dx in range(3):
        parts = [push_ref[dx, k + 1, 1] + push_ref[dx, k, 2] + push_ref[dx, k + 2, 0] if reaches(dx, k) else pad
                 for k in range(blocks)]
        bias.append(jnp.concatenate(parts + [pad], axis=0) * inside[dx])
    ab = [force(bias, dx) for dx in range(3)]
    aab = force(ab, 1)
    basis = [x[here] for x in (vel[1], bias[1], av[1], ab[1], aav, aab)]

    index, sums = {}, []
    for i in range(6):
        for j in range(i, 6):
            index[i, j] = index[j, i] = len(sums)
            sums.append(jnp.sum(basis[i] * basis[j], axis=0, keepdims=True))
    sums = jnp.sum(jnp.concatenate(sums + [jnp.zeros((3, 128), jnp.float32)], axis=0), axis=1, keepdims=True)
    diagonal = lax.broadcasted_iota(jnp.int32, (24, 128), 0) == lax.broadcasted_iota(jnp.int32, (24, 128), 1)
    part2[0] = jnp.sum(jnp.where(diagonal, sums, 0.0), axis=0, keepdims=True)

    def scatter(part, count, peer, sem, got):
        sends = []
        for r in range(1, count):
            sends.append(pltpu.make_async_remote_copy(
                src_ref=part.at[0], dst_ref=part.at[r], send_sem=sem.at[r], recv_sem=got.at[r],
                device_id=peer(r), device_id_type=MESH))
            sends[-1].start()
        return sends

    def collect(part, sends):
        for c in sends:
            c.wait_recv()
        return functools.reduce(jnp.add, [part[r] for r in range(len(sends) + 1)])

    pl.semaphore_wait(known, len(corners + ends))
    sends1 = scatter(part2, groups, along, sem_2, got_2)

    back.wait_recv()

    def flow_at(kind, s, j):
        if (kind, s, "s0") in step_of:
            return flows[step_of[kind, s, f"s{j}"]]
        rows = []
        for d in (1, 2, 3):
            if kind == 1 and (s, d) in SPRINGS_BACK:
                n = SPRINGS_BACK.index((s, d))
                rows.append(back_ref[n:n + 1, :])
            else:
                step = step_of[kind, s, d]
                f = flows[step]
                rows.append(f if STEPS[step][kind] == (kind, s, d) else pltpu.roll(f, 32, axis=1))
        return jnp.where(skip[s][j] == 1, rows[0], jnp.where(skip[s][j] == 2, rows[1], rows[2]))

    for s in range(4):
        for j in range(2):
            f = jnp.where(low, flow_at(0, s, j), flow_at(1, s, j))
            out_ref[2 * s + j:2 * s + j + 1, :] = jnp.where(live[s][j], f, 0.0)

    for i in range(6):
        spectrum_copy(i).wait_send()
    for c in early + late + [back]:
        c.wait_send()
    part1[0] = collect(part2, sends1)
    sends2 = scatter(part1, 4 * nx, near, sem_1, got_1)
    gram = collect(part1, sends2)
    g = {k: jnp.broadcast_to(gram[:, n:n + 1], (1, 128)) for k, n in index.items()}

    def dot(p, q):
        terms = [p[i] * q[j] * g[i, j] for i in range(6) for j in range(6) if p[i] is not None and q[j] is not None]
        return functools.reduce(jnp.add, terms)

    def plus(*xs):
        xs = [x for x in xs if x is not None]
        return functools.reduce(jnp.add, xs) if xs else None

    def times(k, x):
        return None if x is None else k * x

    one = jnp.ones((1, 128), jnp.float32)
    v = [one] + [None] * 5
    d = [None] * 6
    for it in range(ITERS):
        f = [None, one] + d[:4]
        power, speed, strength = dot(f, v), dot(v, v), dot(f, f)
        speed, strength = jnp.maximum(speed, 0.0), jnp.maximum(strength, 0.0)
        gating = 0.5 + 0.5 * power / jnp.sqrt((speed + TINY) * (strength + TINY))
        ratio = jnp.sqrt((speed + TINY) / (strength + TINY))
        mix, step = mix_ref[it], step_ref[it]
        kv, kf = gating * (1.0 - mix), gating * (mix * ratio) + step
        v = [plus(times(kv, v[i]), times(kf, f[i])) for i in range(6)]
        d = [plus(d[i], times(step, v[i])) for i in range(6)]
    result = functools.reduce(jnp.add, [d[i] * basis[i] for i in range(6)])
    out_ref[8:12, :] = result

    for c in sends1 + sends2:
        c.wait_send()


def unpack_kernel(packed_ref, flow_ref, displace_ref):
    for c in range(2):
        for a in range(2):
            lanes = slice(c * 64 + a * 32, c * 64 + a * 32 + 32)
            for s in range(4):
                displace_ref[s, c, a:a + 1, :] = packed_ref[8 + s:9 + s, lanes]
                for j in range(2):
                    flow_ref[s, j, c, a:a + 1, :] = packed_ref[2 * s + j:2 * s + j + 1, lanes]


def body(sections, skips, patch_valid, velocity_start, step_size, mixing):
    nz, nx = lax.axis_size("gz"), lax.axis_size("xy")
    vm, hbm = (pl.BlockSpec(memory_space=k) for k in (pltpu.VMEM, pl.ANY))
    tables = jnp.asarray(host_tables())
    width = sections.shape[2]
    couples = width // 128
    dma = pltpu.SemaphoreType.DMA
    wide, close = len(halo(FAR)), len(halo(NEAR))
    f32, bf16 = jnp.float32, jnp.bfloat16
    vmem = pltpu.VMEM
    packed = pl.pallas_call(
        functools.partial(kernel, nz, nx),
        out_shape=jax.ShapeDtypeStruct((12, 128), f32),
        in_specs=[hbm] * 7, out_specs=vm,
        scratch_shapes=[
            pltpu.SMEM((2, 4), jnp.int32), pltpu.SMEM((3,), f32), pltpu.SMEM((3,), f32),
            vmem(patch_valid.shape, jnp.int32), vmem(velocity_start.shape, f32),
            vmem(sections.shape, bf16), vmem(tables.shape, bf16),
            vmem((8, 1, width), f32), vmem((8, 1, width), f32),
            vmem((64, couples * 256), bf16),
            vmem((8, couples, HALF, 256), bf16), vmem((6, couples, HALF, 256), bf16),
            vmem((64, couples * 256), bf16),
            vmem((len(STEPS) * couples * 32 * 8 // 16, 128), f32), vmem((len(STEPS) * couples * 32 * 8 // 16, 128), f32), vmem((len(STEPS) * couples * 32 * 8 // 16, 128), f32),
            vmem((64, couples * 256), bf16),
            vmem((3, 2 * NEAR + 1, 2, 4, 128), f32), vmem((3, 2 * FAR + 1, 3, 4, 128), f32),
            vmem((6, 128), f32), vmem((6, 128), f32),
            vmem((4 * nx, 1, 128), f32), vmem((nz // 4, 1, 128), f32),
            dma((5,)), dma((8,)), dma, dma((6,)), dma((6,)), dma((close,)), dma((close,)), dma((wide,)), dma((wide,)), dma, dma,
            dma((4 * nx,)), dma((4 * nx,)), dma((nz // 4,)), dma((nz // 4,)),
            pltpu.SemaphoreType.REGULAR,
        ],
        compiler_params=pltpu.CompilerParams(collective_id=0, has_side_effects=True, vmem_limit_bytes=56 * 2**20),
        name="flow_relax",
    )(sections, tables, skips.T, step_size, mixing, patch_valid, velocity_start)
    return pl.pallas_call(
        unpack_kernel,
        out_shape=(jax.ShapeDtypeStruct((4, 2, 2, 2, 32), f32), jax.ShapeDtypeStruct((4, 2, 2, 32), f32)),
        in_specs=[vm], out_specs=(vm, vm), name="unpack",
    )(packed)


def solution(mesh):
    in_specs = (
        P("gz", "xy", None),
        P("gz", None),
        P("gz", "xy", None),
        P("gz", None, "xy", None),
        P(),
        P(),
    )
    out_specs = (P("gz", None, None, "xy", None), P("gz", None, "xy", None))
    return jax.shard_map(body, mesh=mesh, in_specs=in_specs, out_specs=out_specs, check_vma=False)
```

```python
import functools
import jax
import jax.numpy as jnp
import numpy as np
import ml_dtypes
from jax import lax
from jax.experimental import pallas as pl
from jax.experimental.pallas import tpu as pltpu
from jax.sharding import PartitionSpec as P

PATCH = 64
HALF = 32
ITERS = 3
SHARP = 400.0
STIFF = 0.25
TINY = 1e-06
LOG2E = 1.4426950408889634
SCORE_EXP = SHARP / float(PATCH**4) * LOG2E
MESH = pl.DeviceIdType.MESH
EARLY = 5
STEPS = [
    [(0, 0, "s0"), (1, 0, "s0")],
    [(0, 0, "s1"), (1, 0, "s1")],
    [(1, 1, 1), (1, 1, 2)],
    [(0, 1, "s0"), (1, 2, 1)],
    [(0, 1, "s1"), (2, 3, 1)],
    [(0, 3, 1), (2, 3, 2)],
    [(0, 2, "s0"), (2, 3, 3)],
    [(0, 2, "s1"), (2, 2, 2)],
    [(0, 3, 2), (2, 2, 3)],
    [(0, 3, 3), (2, 1, 3)],
]
ARRIVALS = [3, 6, 9]
SEND = 2
SPRINGS_BACK = [(3, 1), (3, 2), (3, 3), (2, 2), (2, 3), (1, 3)]
NEAR, FAR = 2, 3


def host_tables():
    n = np.arange(PATCH)
    angle = ((n[:, None] * n[None, :]) % PATCH) * (2.0 * np.pi / PATCH)
    rounded = lambda a: np.where(np.abs(a) < 1e-9, 0.0, a).astype(ml_dtypes.bfloat16).astype(np.float64)
    cos, sin = rounded(np.cos(angle)), rounded(np.sin(angle))
    z = np.zeros((PATCH, PATCH))
    forward_cols = np.block([[cos, z, sin, z], [z, cos, z, sin]])
    forward_rows = np.concatenate([cos[:32], cos[32:33], sin[1:32]], axis=0)

    def couple(rr, ri, ir, ii):
        return np.block([[rr, z, ri, z], [z, rr, z, ri], [ir, z, ii, z], [z, ir, z, ii]])

    icols = couple(cos, sin, -sin, cos)
    rr, ri, ir, ii = (np.zeros((PATCH, PATCH)) for _ in range(4))
    rr[0] = cos[0]
    rr[1:32] = 2.0 * cos[1:32]
    ir[1:32] = -2.0 * sin[1:32]
    ir[0] = cos[32]
    ri[32] = cos[32]
    ri[33:] = 2.0 * cos[33:]
    ii[33:] = -2.0 * sin[33:]
    ii[32] = cos[0]
    ipack = couple(rr, ri, ir, ii)
    inverse_rows = np.zeros((64, 64))
    inverse_rows[:, 0] = 1.0
    inverse_rows[:, 1:32] = 2.0 * cos[:, 1:32]
    inverse_rows[:, 32] = cos[:, 32]
    inverse_rows[:, 33:] = -2.0 * sin[:, 1:32]
    last = np.concatenate([forward_rows, z, inverse_rows, z], axis=1)
    return np.concatenate([forward_cols, icols, ipack, last], axis=0).astype(ml_dtypes.bfloat16)


def half_sums(v, left):
    a = jnp.sum(jnp.where(left, v, 0.0), axis=1, keepdims=True)
    b = jnp.sum(jnp.where(left, 0.0, v), axis=1, keepdims=True)
    return jnp.where(left, a, b)


def tile_stats(x_ref, s, a, mean_ref, rs_ref, chunk=512):
    rows = pl.ds(pl.multiple_of(a * PATCH, PATCH), PATCH)
    left = lax.broadcasted_iota(jnp.int32, (1, 128), 1) < 64
    t = s * 2 + a
    scale = 1.0 / PATCH**2
    spans = range(0, chunk, 128)
    for c in range(0, x_ref.shape[2], chunk):
        x = x_ref[s, rows, c:c + chunk].astype(jnp.float32)
        total = jnp.sum(x, axis=0, keepdims=True)
        mean = jnp.concatenate([half_sums(total[:, k:k + 128], left) for k in spans], axis=1) * scale
        mean_ref[t, :, c:c + chunk] = mean
        d = x - mean
        total = jnp.sum(d * d, axis=0, keepdims=True)
        spread = jnp.concatenate([half_sums(total[:, k:k + 128], left) for k in spans], axis=1) * scale
        rs_ref[t, :, c:c + chunk] = lax.rsqrt(spread + 1e-5)


def tile_columns(x_ref, s, a, mean_ref, rs_ref, fcols, half_ref):
    rows = pl.ds(pl.multiple_of(a * PATCH, PATCH), PATCH)
    t = s * 2 + a
    for i in range(x_ref.shape[2] // 128):
        cols = slice(i * 128, (i + 1) * 128)
        x = x_ref[s, rows, cols].astype(jnp.float32)
        normed = ((x - mean_ref[t, :, cols]) * rs_ref[t, :, cols]).astype(jnp.bfloat16)
        half_ref[:, i * 256:(i + 1) * 256] = jnp.dot(normed, fcols, preferred_element_type=jnp.float32).astype(jnp.bfloat16)


def tile_rows(s, a, frows, half_ref, spec_ref):
    lane = lax.broadcasted_iota(jnp.int32, (8, 128), 1) % 64
    row0 = lax.broadcasted_iota(jnp.int32, (8, 128), 0) == 0
    upper = lane >= 32
    for i in range(spec_ref.shape[1]):
        both = jnp.dot(frows, half_ref[:, i * 256:(i + 1) * 256], preferred_element_type=jnp.float32)
        ca, cb = both[:HALF, :128], both[:HALF, 128:]
        sa, sb = both[HALF:, :128], both[HALF:, 128:]
        real, imag = ca - sb, sa + cb
        ca, cb, sa, sb = ca[:8], cb[:8], sa[:8], sb[:8]
        real0 = jnp.where(upper, sa, ca)
        imag0 = jnp.where(upper, sb, cb)
        imag0 = jnp.where(lane == 0, pltpu.roll(ca, 96, axis=1), jnp.where(lane == 32, pltpu.roll(sa, 32, axis=1), imag0))
        real = jnp.concatenate([jnp.where(row0, real0, real[:8]), real[8:]], axis=0)
        imag = jnp.concatenate([jnp.where(row0, imag0, imag[:8]), imag[8:]], axis=0)
        spec_ref[s * 2 + a, i] = jnp.concatenate([real, imag], axis=1).astype(jnp.bfloat16)


def pair_cross(tasks, count, icols, ipack, u_ref):
    lane = lax.broadcasted_iota(jnp.int32, (8, 128), 1) % 32
    row = lax.broadcasted_iota(jnp.int32, (8, 128), 0)
    special = (row == 0) & (lane == 0)
    blocks = []
    for mine_of, other_of in tasks:
        for i in range(count):
            mine, other = mine_of(i).astype(jnp.float32), other_of(i).astype(jnp.float32)
            r, m = mine[:, :128], mine[:, 128:]
            p, q = other[:, :128], other[:, 128:]
            rp, mq = r * p, m * q
            real, imag = rp + mq, m * p - r * q
            real = jnp.concatenate([jnp.where(special, rp[:8], real[:8]), real[8:]], axis=0)
            imag = jnp.concatenate([jnp.where(special, mq[:8], imag[:8]), imag[8:]], axis=0)
            blocks.append(jnp.concatenate([real, imag], axis=1).astype(jnp.bfloat16))
    n = len(blocks)
    inner = jnp.dot(jnp.concatenate(blocks, axis=0), icols, preferred_element_type=jnp.float32)
    first = jnp.dot(jnp.concatenate([b[:16] for b in blocks], axis=0), ipack, preferred_element_type=jnp.float32)
    row0 = lax.broadcasted_iota(jnp.int32, (8, 256), 0) == 0
    for i in range(n):
        head = jnp.where(row0, first[i * 16:i * 16 + 8], inner[i * 32:i * 32 + 8])
        u = jnp.concatenate([head, inner[i * 32 + 8:i * 32 + 32]], axis=0).astype(jnp.bfloat16)
        u_ref[:32, i * 128:(i + 1) * 128] = u[:, :128]
        u_ref[32:, i * 128:(i + 1) * 128] = u[:, 128:]


def pair_soft(u_ref, n, irows, m_ref, z_ref, r_ref, step):
    for h in range(0, n, 2):
        corr = jnp.dot(irows, u_ref[:, h * 128:(h + 2) * 128], preferred_element_type=jnp.float32)
        for i in (h, h + 1):
            e = [corr[8 * r:8 * r + 8, (i - h) * 128:(i - h + 1) * 128] for r in range(8)]
            m = functools.reduce(jnp.maximum, e)
            e = [jnp.exp2((v - m) * SCORE_EXP) for v in e]
            s3 = e[3]
            s2 = e[2] + s3
            s1 = e[1] + s2
            t4 = e[4]
            t5 = t4 + e[5]
            t6 = t5 + e[6]
            t7 = t6 + e[7]
            spot = pl.ds(pl.multiple_of((step * n + i) * 8, 8), 8)
            m_ref[spot] = m
            z_ref[spot] = (s1 + e[0]) + t7
            r_ref[spot] = ((s1 + s2) + s3) - ((t4 + t5) + (t6 + t7))


def pair_finish(m_ref, z_ref, r_ref, first, count):
    rows = count * 32
    lane = lax.broadcasted_iota(jnp.int32, (rows, 128), 1)
    left = lane < 64
    t2 = lane % 64
    shift = jnp.where(t2 < 32, t2, t2 - 64).astype(jnp.float32)
    pick = lambda ref, r: ref[pl.ds(first * 256 + r, rows, stride=8), :]
    top = functools.reduce(jnp.maximum, [pick(m_ref, r) for r in range(8)])
    a = jnp.max(jnp.where(left, top, -jnp.inf), axis=1, keepdims=True)
    b = jnp.max(jnp.where(left, -jnp.inf, top), axis=1, keepdims=True)
    peak = jnp.where(left, a, b)
    beyond = jnp.zeros((rows, 128), jnp.float32)
    stairs = jnp.zeros((rows, 128), jnp.float32)
    eights = jnp.zeros((rows, 128), jnp.float32)
    for r in range(7, -1, -1):
        w = jnp.exp2((pick(m_ref, r) - peak) * SCORE_EXP)
        beyond += w * pick(z_ref, r)
        eights += w * pick(r_ref, r)
        if r > 0:
            stairs += beyond
    total, along = beyond, 8.0 * eights + stairs
    across = total * shift

    def sides(v):
        return (jnp.sum(jnp.where(left, v, 0.0), axis=1, keepdims=True), jnp.sum(jnp.where(left, 0.0, v), axis=1, keepdims=True))

    owner = lax.broadcasted_iota(jnp.int32, (rows, 128), 0) % 32
    mine = (lane % 64) // 2 == owner
    odd = lane % 2 == 1
    (tl, tr), (al, ar), (cl, cr) = sides(total), sides(along), sides(across)
    down = jnp.where(mine, jnp.where(odd, tr, tl), 0.0)
    up = jnp.where(mine, jnp.where(left, jnp.where(odd, ar, al), jnp.where(odd, cr, cl)), 0.0)
    fold = lambda v: [jnp.sum(v[k * 32:(k + 1) * 32], axis=0, keepdims=True) for k in range(count)]
    return [u / d for u, d in zip(fold(up), fold(down))]


def halo(reach):
    return [(db, dx) for dx in (0, -1, 1) for db in range(-reach, reach + 1)
            if (db, dx) != (0, 0) and abs(db) + abs(dx) <= reach]


def shifted(x, by):
    return pltpu.roll(x, (-by) % x.shape[0], axis=0)


def kernel(nz, nx, x_hbm, tab_hbm, skip_hbm, step_hbm, mix_hbm, valid_hbm, start_hbm, out_ref,
           skip_ref, step_ref, mix_ref, valid_ref, start_ref, x_ref, tab_ref, mean_ref, rs_ref, half_ref, spec_ref, recv_ref, u_ref, m_ref, z_ref, r_ref,
           u2_ref, ext_ref, push_ref, back_ref, sent_ref, part1, part2,
           sem_in, sem_x, sem_tab, sem_s, got_s, sem_e, got_e, sem_l, got_l, sem_b, got_b, sem_1, got_1, sem_2, got_2, known):
    gz = lax.axis_index("gz")
    xy = lax.axis_index("xy")
    groups = nz // 4
    yy, zc = gz // groups, gz % groups
    couples = spec_ref.shape[1]

    def tile(i):
        half = i // 2
        a = 1 - i % 2
        return half + a * (3 - 2 * half), a

    def tile_load(i):
        s, a = tile(i)
        part = pl.ds(a * PATCH, PATCH)
        return pltpu.make_async_copy(x_hbm.at[s, part], x_ref.at[s, part], sem_x.at[i])

    loads = [tile_load(i) for i in range(8)]
    loads[0].start()
    small = [(skip_hbm, skip_ref), (valid_hbm, valid_ref), (start_hbm, start_ref), (step_hbm, step_ref), (mix_hbm, mix_ref)]
    small = [pltpu.make_async_copy(a, b, sem_in.at[n]) for n, (a, b) in enumerate(small)]
    for c in small + loads[1:]:
        c.start()
    tab_load = pltpu.make_async_copy(tab_hbm, tab_ref, sem_tab)
    tab_load.start()

    def at(db, dx):
        return (lax.rem(gz + db + nz, nz), lax.rem(xy + dx + nx, nx))

    def near(r):
        k = lax.rem(yy * nx + xy + r, 4 * nx)
        return (k // nx * groups + zc, lax.rem(k, nx))

    def along(r):
        return (yy * groups + lax.rem(zc + r, groups), xy)

    wide, close = halo(FAR), halo(NEAR)
    barrier = pltpu.get_barrier_semaphore()
    def plane(dx, dy):
        return (lax.rem(yy + dy + 4, 4) * groups + zc, lax.rem(xy + dx + nx, nx))

    corners = [plane(dx, dy) for dx in (-1, 1) for dy in (-1, 1)]
    ends = [along(r) for r in (4, groups - 4)]
    peers = [at(db, dx) for db, dx in wide] + corners + [plane(0, -1), plane(0, 1)]
    peers += [along(r) for k in range(1, 5) for r in (k, groups - k)]
    for peer in peers:
        pl.semaphore_signal(barrier, inc=1, device_id=peer, device_id_type=MESH)

    for c in small:
        c.wait()
    lanes = lax.broadcasted_iota(jnp.int32, (1, 128), 1)
    skip = [[skip_ref[j, s] for j in range(2)] for s in range(4)]
    live = [[(k > 0) & (gz * 4 + s + k < 4 * nz) for k in skip[s]] for s in range(4)]
    for s in range(4):
        ext_ref[1, NEAR, 0, s:s + 1, :] = jnp.concatenate(
            [start_ref[s, c, a:a + 1, :] for c in range(2) for a in range(2)], axis=1)
        row = jnp.concatenate([valid_ref[s, a:a + 1, :] for a in range(2)] * 2, axis=1).astype(jnp.float32)
        for d in (1, 2, 3):
            hit = ((skip[s][0] == d) & live[s][0]) | ((skip[s][1] == d) & live[s][1])
            row = jnp.where(lanes == 63 + d, jnp.where(hit, 1.0, 0.0), row)
        ext_ref[1, NEAR, 1, s:s + 1, :] = row

    def stats(i):
        tile_stats(x_ref, *tile(i), mean_ref, rs_ref)

    def columns(i):
        tile_columns(x_ref, *tile(i), mean_ref, rs_ref, tab_ref[0:128], half_ref)

    def rows(i):
        tile_rows(*tile(i), tab_ref[640:704, 0:64], half_ref, spec_ref)

    def spectrum_copy(i):
        s, a = tile(i)
        slot = s + 2 * a
        return pltpu.make_async_remote_copy(
            src_ref=spec_ref.at[s * 2 + a], dst_ref=recv_ref.at[slot], send_sem=sem_s.at[slot], recv_sem=got_s.at[slot],
            device_id=(lax.rem(gz + nz - 1 + 2 * a, nz), xy), device_id_type=MESH)

    loads[0].wait()
    stats(0)
    tab_load.wait()
    columns(0)
    rows(0)
    pl.semaphore_wait(barrier, len(peers))
    spectrum_copy(0).start()
    loads[1].wait()
    stats(1)
    columns(1)
    rows(1)
    spectrum_copy(1).start()
    for peer in corners + ends:
        pl.semaphore_signal(known, inc=1, device_id=peer, device_id_type=MESH)
    early = []
    for n, (db, dx) in enumerate(close):
        early.append(pltpu.make_async_remote_copy(
            src_ref=ext_ref.at[1, NEAR], dst_ref=ext_ref.at[dx + 1, db + NEAR], send_sem=sem_e.at[n], recv_sem=got_e.at[n],
            device_id=at(-db, -dx), device_id_type=MESH))
        early[-1].start()
    for c in loads[2:]:
        c.wait()
    stats(2)
    stats(3)
    columns(2)

    def forward(i, _):
        rows(i - 2)
        columns(i - 1)
        stats(i)
        return 0

    lax.fori_loop(4, 8, forward, 0)
    spectrum_copy(2).start()
    spectrum_copy(3).start()
    rows(6)
    columns(7)
    rows(7)

    def own(s, a):
        return lambda i: spec_ref[s * 2 + a, i]

    def got(slot):
        return lambda i: recv_ref[slot, i]

    def task(kind, s, what):
        if kind == 2:
            return got(2 + s), own(s + what - 4, 1)
        if what not in ("s0", "s1"):
            return own(s, kind), got(s + what - 4) if s + what > 3 else own(s + what, kind)
        d = skip_ref[int(what[1]), s]
        if s == 0:
            return own(0, kind), own(d, kind)
        if s == 1:
            inner = own(jnp.minimum(d + 1, 3), kind)
            return own(1, kind), lambda i: jnp.where(d == 3, recv_ref[0, i], inner(i))
        return own(2, kind), lambda i: jnp.where(d == 1, spec_ref[6 + kind, i], jnp.where(d == 2, recv_ref[0, i], recv_ref[1, i]))

    def cross(step):
        pair_cross([task(*t) for t in STEPS[step]], couples, tab_ref[128:384], tab_ref[384:640], (u_ref, u2_ref)[step % 2])

    def soft(step):
        pair_soft((u_ref, u2_ref)[step % 2], 2 * couples, tab_ref[640:704, 128:192], m_ref, z_ref, r_ref, step)

    last = len(STEPS) - 1
    flows = []
    cross(0)
    for step in range(1, last):
        if step in ARRIVALS:
            k = ARRIVALS.index(step)
            spectrum_copy(2 * k).wait_recv()
            spectrum_copy(2 * k + 1).wait_recv()
        if step == SEND:
            spectrum_copy(4).start()
            spectrum_copy(5).start()
        soft(step - 1)
        cross(step)
        if step == EARLY:
            flows += pair_finish(m_ref, z_ref, r_ref, 0, EARLY)

    for c in early:
        c.wait_recv()
    blocks = 2 * NEAR + 1
    size = 4 * blocks + 4
    here = slice(4 * NEAR, 4 * NEAR + 4)
    lane = lax.broadcasted_iota(jnp.int32, (size, 128), 1)
    col = lane % 32
    upper = (lane // 32) % 2 == 0
    inside = [jnp.where(xy > 0, 1.0, 0.0), 1.0, jnp.where(xy < nx - 1, 1.0, 0.0)]
    pad = jnp.zeros((4, 128), jnp.float32)

    def reaches(dx, k):
        return abs(k - NEAR) + abs(dx - 1) <= NEAR

    def gather(dx, f):
        return jnp.concatenate([ext_ref[dx, k, f] if reaches(dx, k) else pad for k in range(blocks)] + [pad], axis=0)

    def springs(dx):
        info = gather(dx, 1)
        valid = jnp.where(lane < 64, info, pltpu.roll(info, 64, axis=1))
        return [info[:, 63 + d:64 + d] * valid * shifted(valid, d) for d in (1, 2, 3)]

    weights = [None, springs(1), None]
    soft(last - 1)
    flows += pair_finish(m_ref, z_ref, r_ref, EARLY, last - EARLY)

    low = (lanes // 32) % 2 == 0
    base = 4 * NEAR
    add = [[jnp.zeros((1, 128), jnp.float32) for _ in range(4)] for _ in range(3)]

    def spring(s, d):
        return weights[1][d - 1][base + s:base + s + 1]

    def push(source, target, value):
        for where, sign in ((source, -1.0), (target, 1.0)):
            add[1 + where // 4][where % 4] += sign * value

    def push_step(step):
        for slot, (kind, s, what) in enumerate(STEPS[step]):
            f = flows[step]
            if slot != min(kind, 1):
                f = pltpu.roll(f, 32, axis=1)
            f = jnp.where(low, f, 0.0) if kind == 0 else jnp.where(low, 0.0, f)
            where = s - 4 if kind == 2 else s
            if what in ("s0", "s1"):
                for d in (1, 2, 3):
                    push(where, where + d, jnp.where(skip[s][int(what[1])] == d, spring(where, d), 0.0) * f)
            else:
                push(where, where + what, spring(where, what) * f)

    for step in range(last):
        push_step(step)

    spectrum_copy(4).wait_recv()
    spectrum_copy(5).wait_recv()
    cross(last)
    soft(last)
    flows += pair_finish(m_ref, z_ref, r_ref, last, 1)
    push_step(last)

    for k in range(3):
        push_ref[1, FAR, k] = jnp.concatenate(add[k], axis=0)
    late = []
    for n, (db, dx) in enumerate(wide):
        reach = abs(db) + abs(dx)
        low_part = 0 if db > 0 or reach < 2 else (1 if reach < 3 else 2)
        high_part = 3 if db < 0 or reach < 2 else (2 if reach < 3 else 1)
        part = pl.ds(low_part, high_part - low_part)
        late.append(pltpu.make_async_remote_copy(
            src_ref=push_ref.at[1, FAR, part], dst_ref=push_ref.at[dx + 1, db + FAR, part],
            send_sem=sem_l.at[n], recv_sem=got_l.at[n], device_id=at(-db, -dx), device_id_type=MESH))
        late[-1].start()

    step_of = {t: step for step, tasks in enumerate(STEPS) for t in tasks}
    for n, (s, d) in enumerate(SPRINGS_BACK):
        sent_ref[n:n + 1, :] = flows[step_of[2, s, d]]
    back = pltpu.make_async_remote_copy(
        src_ref=sent_ref, dst_ref=back_ref, send_sem=sem_b, recv_sem=got_b, device_id=at(-1, 0), device_id_type=MESH)
    back.start()

    weights = [springs(0), weights[1], springs(2)]
    vel = [gather(dx, 0) * inside[dx] for dx in range(3)]

    def force(fields, dx):
        v = fields[dx]
        above = fields[dx - 1] if dx > 0 else jnp.zeros_like(v)
        below = fields[dx + 1] if dx < 2 else jnp.zeros_like(v)
        lateral = jnp.where(col == 0, 0.0, pltpu.roll(v, 1, axis=1)) + jnp.where(col == 31, 0.0, pltpu.roll(v, 127, axis=1))
        down, up = pltpu.roll(v, 32, axis=1), pltpu.roll(v, 96, axis=1)
        vertical = jnp.where(upper, pltpu.roll(above, 96, axis=1) + up, down + pltpu.roll(below, 32, axis=1))
        out = STIFF * (lateral + vertical - 4.0 * v)
        for d in (1, 2, 3):
            pull = weights[dx][d - 1] * (shifted(v, d) - v)
            out += pull - shifted(pull, -d)
        return out * inside[dx]

    av = [force(vel, dx) for dx in range(3)]
    aav = force(av, 1)
    for c in late:
        c.wait_recv()
    bias = []
    for dx in range(3):
        parts = [push_ref[dx, k + 1, 1] + push_ref[dx, k, 2] + push_ref[dx, k + 2, 0] if reaches(dx, k) else pad
                 for k in range(blocks)]
        bias.append(jnp.concatenate(parts + [pad], axis=0) * inside[dx])
    ab = [force(bias, dx) for dx in range(3)]
    aab = force(ab, 1)
    basis = [x[here] for x in (vel[1], bias[1], av[1], ab[1], aav, aab)]

    index, sums = {}, []
    for i in range(6):
        for j in range(i, 6):
            index[i, j] = index[j, i] = len(sums)
            sums.append(jnp.sum(basis[i] * basis[j], axis=0, keepdims=True))
    sums = jnp.sum(jnp.concatenate(sums + [jnp.zeros((3, 128), jnp.float32)], axis=0), axis=1, keepdims=True)
    diagonal = lax.broadcasted_iota(jnp.int32, (24, 128), 0) == lax.broadcasted_iota(jnp.int32, (24, 128), 1)
    part2[0] = jnp.sum(jnp.where(diagonal, sums, 0.0), axis=0, keepdims=True)

    def scatter(part, count, peer, sem, got):
        sends = []
        for r in range(1, count):
            sends.append(pltpu.make_async_remote_copy(
                src_ref=part.at[0], dst_ref=part.at[r], send_sem=sem.at[r], recv_sem=got.at[r],
                device_id=peer(r), device_id_type=MESH))
            sends[-1].start()
        return sends

    def collect(part, sends):
        for c in sends:
            c.wait_recv()
        return functools.reduce(jnp.add, [part[r] for r in range(len(sends) + 1)])

    pl.semaphore_wait(known, len(corners + ends))
    sends1 = scatter(part2, groups, along, sem_2, got_2)

    back.wait_recv()

    def flow_at(kind, s, j):
        if (kind, s, "s0") in step_of:
            return flows[step_of[kind, s, f"s{j}"]]
        rows = []
        for d in (1, 2, 3):
            if kind == 1 and (s, d) in SPRINGS_BACK:
                n = SPRINGS_BACK.index((s, d))
                rows.append(back_ref[n:n + 1, :])
            else:
                step = step_of[kind, s, d]
                f = flows[step]
                rows.append(f if STEPS[step][kind] == (kind, s, d) else pltpu.roll(f, 32, axis=1))
        return jnp.where(skip[s][j] == 1, rows[0], jnp.where(skip[s][j] == 2, rows[1], rows[2]))

    for s in range(4):
        for j in range(2):
            f = jnp.where(low, flow_at(0, s, j), flow_at(1, s, j))
            out_ref[2 * s + j:2 * s + j + 1, :] = jnp.where(live[s][j], f, 0.0)

    for i in range(6):
        spectrum_copy(i).wait_send()
    for c in early + late + [back]:
        c.wait_send()
    part1[0] = collect(part2, sends1)
    sends2 = scatter(part1, 4 * nx, near, sem_1, got_1)
    gram = collect(part1, sends2)
    g = {k: jnp.broadcast_to(gram[:, n:n + 1], (1, 128)) for k, n in index.items()}

    def dot(p, q):
        terms = [p[i] * q[j] * g[i, j] for i in range(6) for j in range(6) if p[i] is not None and q[j] is not None]
        return functools.reduce(jnp.add, terms)

    def plus(*xs):
        xs = [x for x in xs if x is not None]
        return functools.reduce(jnp.add, xs) if xs else None

    def times(k, x):
        return None if x is None else k * x

    one = jnp.ones((1, 128), jnp.float32)
    v = [one] + [None] * 5
    d = [None] * 6
    for it in range(ITERS):
        f = [None, one] + d[:4]
        power, speed, strength = dot(f, v), dot(v, v), dot(f, f)
        speed, strength = jnp.maximum(speed, 0.0), jnp.maximum(strength, 0.0)
        gating = 0.5 + 0.5 * power / jnp.sqrt((speed + TINY) * (strength + TINY))
        ratio = jnp.sqrt((speed + TINY) / (strength + TINY))
        mix, step = mix_ref[it], step_ref[it]
        kv, kf = gating * (1.0 - mix), gating * (mix * ratio) + step
        v = [plus(times(kv, v[i]), times(kf, f[i])) for i in range(6)]
        d = [plus(d[i], times(step, v[i])) for i in range(6)]
    result = functools.reduce(jnp.add, [d[i] * basis[i] for i in range(6)])
    out_ref[8:12, :] = result

    for c in sends1 + sends2:
        c.wait_send()


def unpack_kernel(packed_ref, flow_ref, displace_ref):
    for c in range(2):
        for a in range(2):
            lanes = slice(c * 64 + a * 32, c * 64 + a * 32 + 32)
            for s in range(4):
                displace_ref[s, c, a:a + 1, :] = packed_ref[8 + s:9 + s, lanes]
                for j in range(2):
                    flow_ref[s, j, c, a:a + 1, :] = packed_ref[2 * s + j:2 * s + j + 1, lanes]


def body(sections, skips, patch_valid, velocity_start, step_size, mixing):
    nz, nx = lax.axis_size("gz"), lax.axis_size("xy")
    vm, hbm = (pl.BlockSpec(memory_space=k) for k in (pltpu.VMEM, pl.ANY))
    tables = jnp.asarray(host_tables())
    width = sections.shape[2]
    couples = width // 128
    dma = pltpu.SemaphoreType.DMA
    wide, close = len(halo(FAR)), len(halo(NEAR))
    f32, bf16 = jnp.float32, jnp.bfloat16
    vmem = pltpu.VMEM
    packed = pl.pallas_call(
        functools.partial(kernel, nz, nx),
        out_shape=jax.ShapeDtypeStruct((12, 128), f32),
        in_specs=[hbm] * 7, out_specs=vm,
        scratch_shapes=[
            pltpu.SMEM((2, 4), jnp.int32), pltpu.SMEM((3,), f32), pltpu.SMEM((3,), f32),
            vmem(patch_valid.shape, jnp.int32), vmem(velocity_start.shape, f32),
            vmem(sections.shape, bf16), vmem(tables.shape, bf16),
            vmem((8, 1, width), f32), vmem((8, 1, width), f32),
            vmem((64, couples * 256), bf16),
            vmem((8, couples, HALF, 256), bf16), vmem((6, couples, HALF, 256), bf16),
            vmem((64, couples * 256), bf16),
            vmem((len(STEPS) * couples * 32 * 8 // 16, 128), f32), vmem((len(STEPS) * couples * 32 * 8 // 16, 128), f32), vmem((len(STEPS) * couples * 32 * 8 // 16, 128), f32),
            vmem((64, couples * 256), bf16),
            vmem((3, 2 * NEAR + 1, 2, 4, 128), f32), vmem((3, 2 * FAR + 1, 3, 4, 128), f32),
            vmem((6, 128), f32), vmem((6, 128), f32),
            vmem((4 * nx, 1, 128), f32), vmem((nz // 4, 1, 128), f32),
            dma((5,)), dma((8,)), dma, dma((6,)), dma((6,)), dma((close,)), dma((close,)), dma((wide,)), dma((wide,)), dma, dma,
            dma((4 * nx,)), dma((4 * nx,)), dma((nz // 4,)), dma((nz // 4,)),
            pltpu.SemaphoreType.REGULAR,
        ],
        compiler_params=pltpu.CompilerParams(collective_id=0, has_side_effects=True, vmem_limit_bytes=56 * 2**20),
        name="flow_relax",
    )(sections, tables, skips.T, step_size, mixing, patch_valid, velocity_start)
    return pl.pallas_call(
        unpack_kernel,
        out_shape=(jax.ShapeDtypeStruct((4, 2, 2, 2, 32), f32), jax.ShapeDtypeStruct((4, 2, 2, 32), f32)),
        in_specs=[vm], out_specs=(vm, vm), name="unpack",
    )(packed)


def solution(mesh):
    in_specs = (
        P("gz", "xy", None),
        P("gz", None),
        P("gz", "xy", None),
        P("gz", None, "xy", None),
        P(),
        P(),
    )
    out_specs = (P("gz", None, None, "xy", None), P("gz", None, "xy", None))
    return jax.shard_map(body, mesh=mesh, in_specs=in_specs, out_specs=out_specs, check_vma=False)
```
